256 devices in a mesh: sub: 32 (over z, x), loc: 8 (over y, core).
Axes of the slice: x: 4, y: 4, z: 8, core: 2. Of those that a mesh axis runs over, the one named last changes fastest.
Arguments:
- partials: float32 [512, 8, 128, 256], P('sub', None, 'loc'), may hold values from -20 to 20
- local_schur: float32 [512, 8, 128, 1024], P('sub', None, 'loc'), may hold values from -1 to 2
- rigid_basis: float32 [512, 6, 8, 128], P('sub', None, None, 'loc'), may hold values from -0.1875 to 0.1875
- coarse_inverse: float32 [1536, 1536], P('sub', 'loc'), may hold values from -1 to 1
- placement: int32 [32], replicated, may hold values from 1 to 13, 160 in all
- neighbour_sub: int32 [256, 8], replicated, may hold values from -1 to 255, as said below
- neighbour_tile: int32 [256, 8], replicated, may hold values from -1 to 7, as said below
- coarse_number: int32 [1536], replicated, may hold values from 0 to 1535, each once
Outputs:
- precond: float32 [512, 8, 128, 256], P('sub', None, 'loc')
- inner_sums: float32 [256], replicated
The draws below stay inside these ranges and needn't reach their ends.
Inputs may be any that keep to these rules, and one draw needn't show every extreme that they name: Owner o holds placement[o] + 3 subdomains. Where neighbour_sub[s, t] = s2 >= 0: s2 != s, |s2 - s| <= 4, neighbour_sub[s2, neighbour_tile[s, t]] = s and neighbour_tile[s2, neighbour_tile[s, t]] = t; no two tiles of s share one tile of s2. neighbour_tile is -1 exactly where neighbour_sub is. `coarse_number`: each coarse unknown once.
All inputs are finite; a program needn't handle non-finite values.
Results may differ from the reference program's by a relative error of at most 0.000054.
Values sent between devices are 32-bit elements; how exact they have to be, the bound alone decides.
A program may use at most 128 MiB of HBM per device.

```python
import math
import jax
import jax.numpy as jnp
import numpy as np
from jax import lax

TILE_ROWS = 128
TILES = 8
MODES = 6
SLAB = 4
SUB_DEV = 8
NRHS = 256
SLOTS = 16
SUBS = 256
SL_ALL = 512
NC = 1536
N_SUB = 32


def neighbour_tables(key):
    sub_ids = jnp.arange(SUBS, dtype=jnp.int32)
    sub_keys = jax.random.split(jax.random.fold_in(key, 11), SUBS)
    orders = jax.vmap(lambda sub_key: jax.random.permutation(sub_key, TILES))(sub_keys).astype(jnp.int32)
    keep_draw = jax.random.randint(jax.random.fold_in(key, 12), (SUBS, 5), 0, 4)
    mate_lists = [jnp.bitwise_xor(sub_ids, 1), jnp.bitwise_xor(sub_ids, 2), sub_ids - SLAB, sub_ids + SLAB, jnp.bitwise_xor(sub_ids, 3)]
    back_role = [0, 1, 3, 2, 4]
    canon_role = [0, 1, 2, 2, 4]
    sub_table = jnp.full((SUBS, TILES), -1, jnp.int32)
    tile_table = jnp.full((SUBS, TILES), -1, jnp.int32)
    for role_index in range(5):
        inside = (mate_lists[role_index] >= 0) & (mate_lists[role_index] < SUBS)
        mate_ids = jnp.clip(mate_lists[role_index], 0, SUBS - 1)
        lower_id = jnp.minimum(sub_ids, mate_ids)
        kept_pair = inside & ((keep_draw[lower_id, canon_role[role_index]] != 0) | (role_index == 4))
        sub_table = sub_table.at[sub_ids, orders[:, role_index]].set(jnp.where(kept_pair, mate_ids, -1))
        tile_table = tile_table.at[sub_ids, orders[:, role_index]].set(jnp.where(kept_pair, orders[mate_ids, back_role[role_index]], -1))
    return (sub_table, tile_table)


def draw_neighbour_sub(key, part):
    shared_tables = neighbour_tables(key)
    return shared_tables[0]


def draw_neighbour_tile(key, part):
    shared_tables = neighbour_tables(key)
    return shared_tables[1]


def draw_partials(key, part):
    key = jax.random.fold_in(key, 5)
    full_shape = (SL_ALL, TILES, TILE_ROWS, NRHS)
    position = jnp.arange(SL_ALL, dtype=jnp.float32) / (SL_ALL - 1)
    rising = 1.0 + 2.0 * position
    values = jnp.clip(jax.random.normal(key, full_shape, jnp.float32), -5.0, 5.0)
    return values * rising[:, None, None, None]


def draw_local_schur(key, part):
    key = jax.random.fold_in(key, 7)
    matrix_order = TILES * TILE_ROWS
    full_shape = (SL_ALL, TILES, TILE_ROWS, matrix_order)
    row_ids = lax.broadcasted_iota(jnp.int32, (1, TILES, TILE_ROWS, 1), 1) * TILE_ROWS + lax.broadcasted_iota(jnp.int32, (1, TILES, TILE_ROWS, 1), 2)
    col_ids = lax.broadcasted_iota(jnp.int32, (1, 1, 1, matrix_order), 3)
    diagonal = 1.0 + 0.5 * jax.random.uniform(jax.random.fold_in(key, 1), (SL_ALL, TILES, TILE_ROWS, 1), jnp.float32)
    off_diagonal = jnp.clip(jax.random.normal(key, full_shape, jnp.float32), -5.0, 5.0)
    return jnp.where(row_ids == col_ids, diagonal, 0.0) + 0.5 / math.sqrt(matrix_order) * off_diagonal


def levels(key, shape, shards, low, top_value):
    factor_of, own = 1.0, jax.random.fold_in(key, 6)
    for axis_at, blocks in shards:
        steps = jnp.exp(jax.random.uniform(jax.random.fold_in(own, axis_at), (blocks,), jnp.float32, low / len(shards), top_value / len(shards)))
        factor_of = factor_of * jnp.repeat(steps, shape[axis_at] // blocks).reshape([-1 if axis == axis_at else 1 for axis in range(len(shape))])
    return factor_of


def split_up(count, total, bound, skew):
    loads = [(1 << 20) // math.isqrt(grade ** skew) + 1 for grade in range(2, count + 1)]
    spare, counts = total - bound - (count - 1), [1] * (count - 1)
    while spare > 0:
        candidates = [i for i in range(count - 1) if counts[i] < bound]
        pool, remaining = sum([loads[i] for i in candidates]), spare
        for i in candidates:
            extra = min(bound - counts[i], max(1, remaining * loads[i] // pool), spare)
            counts[i] = counts[i] + extra
            spare = spare - extra
    return np.array([bound] + counts)


def ragged_sizes(stream_key, count, total, reach, lean):
    if count == 2:
        one = jax.random.randint(stream_key, (), max(1, total - reach), min(reach, total - 1) + 1)
        return jnp.stack([one, total - one])
    sizes = jnp.asarray(split_up(count, total, reach, lean), jnp.int32)
    twos = (count - 1) // 2
    source_of, receiver = sizes[1:1 + 2 * twos:2], sizes[2:2 + 2 * twos:2]
    room = jnp.minimum(source_of - 1, reach - receiver)
    passed = jax.random.randint(jax.random.fold_in(stream_key, 1), (twos,), 0, 1 << 20) % (room + 1)
    sizes = sizes.at[1:1 + 2 * twos:2].set(source_of - passed).at[2:2 + 2 * twos:2].set(receiver + passed)
    return sizes[jax.random.permutation(jax.random.fold_in(stream_key, 2), count)]


def scatter_about(stream_key, shape, spread, reach, pieces=(), kind=jnp.bfloat16):
    gain = levels(stream_key, shape, pieces, -0.22, 0.18) if pieces else 1.0
    entries = jax.random.normal(stream_key, shape, jnp.float32) * spread * gain
    return jnp.minimum(jnp.maximum(entries, -reach), reach).astype(kind)


def setup_inputs(seed: int = 0) -> dict:
    key_list = jax.random.split(jax.random.key(seed), 9)
    partials = draw_partials(jax.random.fold_in(key_list[8], 71), 0)
    local_schur = draw_local_schur(jax.random.fold_in(key_list[8], 71), 0)
    rigid_basis = scatter_about(key_list[2], (SL_ALL, MODES, TILES, TILE_ROWS), (TILES * TILE_ROWS) ** -0.5, 0.1875, ((0, 32), (3, 8)), jnp.float32)
    coarse_inverse = scatter_about(key_list[3], (NC, NC), (NC // 36) ** -0.5, 1.0, ((0, 32), (1, 8)), jnp.float32)
    placement = ragged_sizes(key_list[4], N_SUB, (SUB_DEV - SLAB + 1) * N_SUB, SLOTS - SLAB + 1, 2).astype(jnp.int32)
    neighbour_sub = draw_neighbour_sub(jax.random.fold_in(key_list[8], 71), 0)
    neighbour_tile = draw_neighbour_tile(jax.random.fold_in(key_list[8], 71), 0)
    coarse_number = jax.random.permutation(key_list[7], NC).astype(jnp.int32)
    return dict(partials=partials, local_schur=local_schur, rigid_basis=rigid_basis, coarse_inverse=coarse_inverse, placement=placement, neighbour_sub=neighbour_sub, neighbour_tile=neighbour_tile, coarse_number=coarse_number)


precise = lax.Precision.HIGHEST


def slot_frame(placement):
    owner_load = placement + (SLAB - 1)
    starts = jnp.cumsum(owner_load) - owner_load
    slot_ids = jnp.arange(SLOTS, dtype=jnp.int32)
    global_id = (starts[:, None] + slot_ids[None, :]).reshape(-1)
    live_slot = (slot_ids[None, :] < owner_load[:, None]).reshape(-1)
    return jnp.minimum(global_id, SUBS - 1).astype(jnp.int32), live_slot


def assemble(values, neighbour_sub, neighbour_tile):
    linked = neighbour_sub >= 0
    mate_ids = jnp.where(linked, neighbour_sub, 0).astype(jnp.int32)
    their_tile = jnp.where(linked, neighbour_tile, 0).astype(jnp.int32)
    mate_values = values[mate_ids, their_tile]
    return values + jnp.where(linked[:, :, None, None], mate_values, jnp.zeros_like(mate_values))


def reference(partials, local_schur, rigid_basis, coarse_inverse, placement, neighbour_sub, neighbour_tile, coarse_number):
    global_id, live_slot = slot_frame(placement)
    targets = jnp.where(live_slot, global_id, SUBS).astype(jnp.int32)
    slot_of = jnp.zeros((SUBS,), jnp.int32).at[targets].set(jnp.arange(SL_ALL, dtype=jnp.int32), mode="drop")
    residual = assemble(partials[slot_of], neighbour_sub, neighbour_tile)
    weight = jnp.where(neighbour_sub >= 0, 0.5, 1.0).astype(jnp.float32)[:, :, None, None]
    scaled = weight * residual
    matrix_order = TILES * TILE_ROWS

    def local_apply(sub_id):
        matrix = local_schur[slot_of[sub_id]].reshape(matrix_order, matrix_order)
        return jnp.dot(matrix, scaled[sub_id].reshape(matrix_order, NRHS), precision=precise, preferred_element_type=jnp.float32)

    applied = lax.map(local_apply, jnp.arange(SUBS, dtype=jnp.int32)).reshape(SUBS, TILES, TILE_ROWS, NRHS)
    coarse_basis = rigid_basis[slot_of]
    coarse_part = jnp.einsum("smtr,strn->smn", coarse_basis, scaled, precision=precise)
    coarse_rhs = jnp.zeros((NC, NRHS), jnp.float32).at[coarse_number].set(coarse_part.reshape(NC, NRHS))
    coarse_solution = jnp.dot(coarse_inverse, coarse_rhs, precision=precise, preferred_element_type=jnp.float32)
    mode_values = coarse_solution[coarse_number].reshape(SUBS, MODES, NRHS)
    corrected = applied + jnp.einsum("smtr,smn->strn", coarse_basis, mode_values, precision=precise)
    assembled = assemble(weight * corrected, neighbour_sub, neighbour_tile)
    inner_sums = jnp.sum(weight * residual * assembled, axis=(0, 1, 2))
    precond = jnp.where(live_slot[:, None, None, None], assembled[global_id], jnp.zeros((), jnp.float32))
    return precond, inner_sums
```

```python
import functools
import jax
import jax.numpy as jnp
from jax import lax
from jax.experimental import pallas as pl
from jax.experimental.pallas import tpu as pltpu
from jax.sharding import PartitionSpec as P

SLAB = 4
X = 4
MESH = pl.DeviceIdType.MESH
HI = lax.Precision.HIGHEST
F32 = jnp.float32


def dot(a, b, dims=(((1,), (0,)), ((), ()))):
    return lax.dot_general(a, b, dims, precision=HI, preferred_element_type=F32)


def kernel(
    n_sub,
    n_loc,
    part_hbm,
    schur_hbm,
    basis,
    inv,
    placement,
    nsub,
    ntile,
    cnum,
    out,
    inner_out,
    PV,
    SV,
    SC,
    G,
    V,
    H1,
    H2,
    SB1,
    SB2,
    CP,
    CT,
    R1,
    R2,
    R3,
    M4,
    MV,
    IF,
    IT,
    W,
    IS1,
    IS2,
    IS3,
    ACC,
    ld,
    hs,
    hr,
    cs,
    cr,
    ysend,
    ra,
    rb,
    ha,
    hb,
    rs,
):
    Z = n_sub // X
    Y = n_loc // 2
    slots, tiles, rl, cols = PV.shape
    subs = nsub.shape[1]
    rows_here = tiles * rl
    modes = 6
    pad = 8
    nb = cols // n_loc
    io, ic = inv.shape

    o = lax.axis_index("sub")
    l = lax.axis_index("loc")
    z, x = o // X, o % X
    y, c = l // 2, l % 2
    lp = 2 * ((y + 1) % Y) + c
    lm = 2 * ((y + Y - 1) % Y) + c
    l2 = 2 * ((y + 2) % Y) + c
    sib = 2 * y + (1 - c)
    right, left = (o + 1) % n_sub, (o + n_sub - 1) % n_sub

    def rcopy(src, dst, send, recv, dev):
        return pltpu.make_async_remote_copy(
            src_ref=src, dst_ref=dst, send_sem=send, recv_sem=recv, device_id=dev, device_id_type=MESH
        )

    def wait_recv(ref, sem):
        rcopy(ref, ref, sem, sem, (o, sib)).wait_recv()

    def wait_send(ref, sem):
        rcopy(ref, ref, sem, sem, (o, sib)).wait_send()

    load_p = pltpu.make_async_copy(part_hbm, PV, ld.at[0])
    load_s = pltpu.make_async_copy(schur_hbm, SV, ld.at[1])
    load_p.start()
    load_s.start()

    barrier = pltpu.get_barrier_semaphore()
    peers = [(right, l), (left, l)]
    peers += [(o, (l + i) % n_loc) for i in range(1, n_loc)]
    peers += [(z * X + (x + i) % X, l) for i in range(1, X)]
    peers += [(((z + i) % Z) * X + x, l) for i in range(1, Z)]
    for peer in peers:
        pl.semaphore_signal(barrier, inc=1, device_id=peer, device_id_type=MESH)

    def load_of(i):
        return placement[i] + (SLAB - 1)

    start = lax.fori_loop(
        0, n_sub, lambda i, acc: acc + jnp.where(i < o, load_of(i), 0), jnp.int32(0)
    )
    cnt = load_of(o)

    def slot_of(p):
        group, i = p // 4, p % 4
        inner = jnp.where(group == 0, 4, 8) + i
        j_right = cnt - 4 + i
        slot = jnp.where(group == 1, j_right, jnp.where(group == 2, i, inner))
        live = jnp.where(group == 1, j_right >= 4, (group == 2) | (inner < cnt - 4))
        return jnp.clip(slot, 0, slots - 1), live

    def pos_of(j):
        p = jnp.where(
            j < 4,
            8 + j,
            jnp.where(j >= cnt - 4, 4 + j - (cnt - 4), jnp.where(j < 8, j - 4, j + 4)),
        )
        return jnp.clip(p, 0, slots - 1)

    def link(j, live, t):
        sid = jnp.clip(start + j, 0, subs - 1)
        partner = nsub[t, sid]
        mate = jnp.clip(ntile[t, sid], 0, tiles - 1)
        linked = (partner >= 0) & live
        q = partner - start
        own = (q >= 0) & (q < cnt)
        hq = jnp.clip(jnp.where(q < 0, 4 + q, 4 + q - cnt), 0, 7)
        return linked, own, jnp.clip(q, 0, slots - 1), hq, mate

    def residual(p, halo):
        j, live = slot_of(p)
        for t in range(tiles):
            linked, own, q, hq, mt = link(j, live, t)
            other = PV[q, mt]
            if halo:
                other = jnp.where(own, other, H1[hq, mt])
            res = PV[j, t] + jnp.where(linked, other, 0.0)
            w = jnp.where(linked, 0.5, 1.0)
            val = jnp.where(live, w * res, 0.0)
            SC[p, t] = val
            G[p, t, l] = val

    def send_own(p):
        src = SC.at[p]
        dst = G.at[p, :, l]
        rcopy(src, dst, ysend, ra.at[p], (o, lp)).start()
        rcopy(src, dst, ysend, rb.at[p], (o, lm)).start()
        rcopy(src, dst, ysend, rs.at[p], (o, sib)).start()

    def forward(p):
        wait_recv(G.at[p, :, lm], ra.at[p])
        half = G.at[p, : tiles // 2, lm]
        rcopy(half, half, ysend, ha.at[p], (o, lp)).start()
        whole = G.at[p, :, lm]
        rcopy(whole, whole, ysend, rs.at[p], (o, sib)).start()
        wait_recv(G.at[p, :, lp], rb.at[p])
        half = G.at[p, tiles // 2 :, lp]
        rcopy(half, half, ysend, hb.at[p], (o, lm)).start()
        whole = G.at[p, :, lp]
        rcopy(whole, whole, ysend, rs.at[p], (o, sib)).start()

    def halves(p):
        wait_recv(G.at[p, : tiles // 2, l2], ha.at[p])
        wait_recv(G.at[p, tiles // 2 :, l2], hb.at[p])
        whole = G.at[p, :, l2]
        rcopy(whole, whole, ysend, rs.at[p], (o, sib)).start()

    def apply_local(p):
        wait_recv(G.at[p, :, : n_loc // 2], rs.at[p])
        j, _ = slot_of(p)
        a = SV[j].reshape(rows_here, tiles * n_loc * rl)
        b = G[p].reshape(tiles * n_loc * rl, cols)
        V[p] = dot(a, b).reshape(tiles, rl, cols)

    def correct(p):
        j, live = slot_of(p)
        corr = dot(basis[j], MV[j], (((0,), (0,)), ((), ())))
        val = V[p] + corr.reshape(tiles, rl, cols)
        acc = ACC[...]
        for t in range(tiles):
            linked, _, _, _, _ = link(j, live, t)
            w = jnp.where(linked, 0.5, 1.0)
            acc = acc + SC[p, t] * val[t]
            V[p, t] = jnp.where(live, w * val[t], 0.0)
        ACC[...] = acc

    def loc_spread(src_of, buf, k):
        for i in range(1, n_loc):
            peer = (l + i) % n_loc
            rcopy(src_of(peer), buf.at[l], cs.at[k], cr.at[k], (o, peer)).start()

    def loc_wait(buf, k):
        wait_recv(buf.at[: n_loc - 1], cr.at[k])

    def x_spread(buf, k):
        for i in range(1, X):
            peer = z * X + (x + i) % X
            rcopy(buf.at[o], buf.at[o], cs.at[k], cr.at[k], (peer, l)).start()

    def x_wait(buf, k):
        wait_recv(buf.at[: X - 1], cr.at[k])

    def z_spread(buf, k):
        block = buf.at[pl.ds(z * X, X)]
        for i in range(1, Z):
            peer = ((z + i) % Z) * X + x
            rcopy(block, block, cs.at[k], cr.at[k], (peer, l)).start()

    def z_wait(buf, k):
        wait_recv(buf.at[: (Z - 1) * X], cr.at[k])

    load_p.wait()

    for i in range(4):
        for t in range(tiles):
            SB1[i, t] = PV[jnp.clip(cnt - 4 + i, 0, slots - 1), t]

    pl.semaphore_wait(barrier, len(peers))

    to_left = rcopy(PV.at[:4], H1.at[4:], hs.at[0], hr.at[0], (left, l))
    to_right = rcopy(SB1, H1.at[:4], hs.at[1], hr.at[1], (right, l))
    to_left.start()
    to_right.start()
    IF[l] = inv[...]
    loc_spread(lambda peer: inv, IF, 0)

    def first(p, carry):
        residual(p, False)
        send_own(p)
        return carry

    lax.fori_loop(0, 4, first, 0)

    def second(p, carry):
        residual(p, False)
        return carry

    lax.fori_loop(12, 16, second, 0)

    ACC[...] = jnp.zeros_like(ACC)
    IT[...] = jnp.zeros_like(IT)
    W[...] = jnp.zeros_like(W)
    loc_wait(IF, 0)
    for k in range(n_loc):
        IT[k * ic : (k + 1) * ic, :io] = IF[k].T

    def fill(s, carry):
        for m in range(modes):
            row = jnp.clip(cnum[s * modes + m], 0, n_loc * ic - 1)
            W[s, m : m + 1, :] = IT[pl.ds(row, 1), :]
        return carry

    lax.fori_loop(0, subs, fill, 0)

    to_left.wait_recv()
    to_right.wait_recv()

    def third(p, carry):
        residual(p, True)
        send_own(p)
        return carry

    lax.fori_loop(4, 12, third, 0)

    def fourth(p, carry):
        send_own(p)
        return carry

    lax.fori_loop(12, 16, fourth, 0)

    def coarse_part(j, carry):
        vals = SC[pos_of(j)].reshape(rows_here, cols)
        vals = jnp.where(j < cnt, vals, 0.0)
        CP[j] = dot(basis[j], vals)
        return carry

    lax.fori_loop(0, slots, coarse_part, 0)
    CT[...] = CP[...].reshape(slots * pad, cols).T.reshape(n_loc, nb, slots * pad)
    R1[l] = CT[l]
    loc_spread(lambda peer: CT.at[peer], R1, 1)

    def reduce_loc():
        loc_wait(R1, 1)
        total = R1[0]
        for i in range(1, n_loc):
            total = total + R1[i]
        R2[o] = total
        x_spread(R2, 2)

    def gather_z():
        x_wait(R2, 2)
        z_spread(R2, 3)

    def solve():
        z_wait(R2, 3)

        def body(k, carry):
            total, at = carry
            rows = W[pl.ds(jnp.clip(at, 0, subs), slots)].reshape(slots * pad, 128)
            total = total + dot(R2[k], rows)
            return total, at + load_of(k)

        total, _ = lax.fori_loop(0, n_sub, body, (jnp.zeros((nb, 128), F32), jnp.int32(0)))
        R3[o] = total
        x_spread(R3, 4)

    def gather_z2():
        x_wait(R3, 4)
        z_spread(R3, 5)

    def select():
        z_wait(R3, 5)
        lanes = lax.broadcasted_iota(jnp.int32, (8, 128), 1)

        def number(j, v):
            sid = jnp.clip(start + j, 0, subs - 1)
            for m in range(modes):
                row = cnum[sid * modes + m]
                v = jnp.where((lanes == j * pad + m) & (j < cnt), row, v)
            return v

        numbers = lax.fori_loop(0, slots, number, jnp.full((8, 128), -1, jnp.int32))
        wanted = jnp.broadcast_to(numbers[:1], (128, 128))
        rows = lax.broadcasted_iota(jnp.int32, (128, 128), 0)

        def body(k, total):
            hot = ((wanted == rows + k * io) & (rows < io)).astype(F32).astype(jnp.bfloat16)
            v = R3[k]
            h = v.astype(jnp.bfloat16)
            r = v - h.astype(F32)
            m = r.astype(jnp.bfloat16)
            q = (r - m.astype(F32)).astype(jnp.bfloat16)
            for part in (h, m, q):
                total = total + lax.dot_general(
                    part, hot, (((1,), (0,)), ((), ())), preferred_element_type=F32
                )
            return total

        mv = lax.fori_loop(0, n_sub, body, jnp.zeros((nb, 128), F32))
        M4[l] = mv
        loc_spread(lambda peer: M4.at[l], M4, 6)

    MV_AT = 10

    def modes_ready():
        loc_wait(M4, 6)
        MV[...] = M4[...].reshape(cols, 128).T.reshape(slots, pad, cols)

        def body(p, carry):
            correct(p)
            return carry

        lax.fori_loop(0, MV_AT - 1, body, 0)

    def send_halo():
        for i in range(4):
            p = pos_of(cnt - 4 + i)
            for t in range(tiles):
                SB2[i, t] = V[p, t]
        rcopy(V.at[8:12], H2.at[4:], hs.at[2], hr.at[2], (left, l)).start()
        rcopy(SB2, H2.at[:4], hs.at[3], hr.at[3], (right, l)).start()

    chain = {2: reduce_loc, 3: gather_z, 4: solve, 5: gather_z2, 6: select, MV_AT: modes_ready, 13: send_halo}

    load_s.wait()

    def step(s, carry):
        @pl.when(s < slots)
        def _():
            forward(s)

        @pl.when((s >= 1) & (s < slots + 1))
        def _():
            halves(s - 1)

        @pl.when(s >= 2)
        def _():
            apply_local(s - 2)

        @pl.when(s > MV_AT)
        def _():
            correct(s - 2)

        for at, what in chain.items():
            pl.when(s == at)(what)
        return carry

    lax.fori_loop(0, slots + 2, step, 0)

    IS1[l] = ACC[: rl // 2, :] + ACC[rl // 2 :, :]
    loc_spread(lambda peer: IS1.at[l], IS1, 7)

    wait_recv(H2.at[4:], hr.at[2])
    wait_recv(H2.at[:4], hr.at[3])

    def finish(j, carry):
        live = j < cnt
        p = pos_of(j)
        for t in range(tiles):
            linked, own, q, hq, mt = link(j, live, t)
            other = jnp.where(own, V[pos_of(q), mt], H2[hq, mt])
            val = V[p, t] + jnp.where(linked, other, 0.0)
            out[j, t] = jnp.where(live, val, 0.0)
        return carry

    lax.fori_loop(0, 6, finish, 0)
    loc_wait(IS1, 7)
    total = IS1[0]
    for i in range(1, n_loc):
        total = total + IS1[i]
    IS2[x] = total
    for i in range(1, X):
        peer = z * X + (x + i) % X
        rcopy(IS2.at[x], IS2.at[x], cs.at[8], cr.at[8], (peer, l)).start()
    lax.fori_loop(6, 11, finish, 0)
    wait_recv(IS2.at[: X - 1], cr.at[8])
    total = IS2[0]
    for i in range(1, X):
        total = total + IS2[i]
    IS3[z] = total
    for i in range(1, Z):
        peer = ((z + i) % Z) * X + x
        rcopy(IS3.at[z], IS3.at[z], cs.at[9], cr.at[9], (peer, l)).start()
    lax.fori_loop(11, 16, finish, 0)
    wait_recv(IS3.at[: Z - 1], cr.at[9])
    total = IS3[0]
    for i in range(1, Z):
        total = total + IS3[i]
    inner_out[...] = jnp.sum(total, axis=0, keepdims=True)

    wait_send(PV.at[:4], hs.at[0])
    wait_send(SB1, hs.at[1])
    wait_send(V.at[8:12], hs.at[2])
    wait_send(SB2, hs.at[3])
    wait_send(G.at[:, :, : n_loc - 1], ysend)
    wait_send(IF.at[: n_loc - 1], cs.at[0])
    wait_send(R1.at[: n_loc - 1], cs.at[1])
    wait_send(R2.at[: X - 1], cs.at[2])
    wait_send(R2.at[: (Z - 1) * X], cs.at[3])
    wait_send(R3.at[: X - 1], cs.at[4])
    wait_send(R3.at[: (Z - 1) * X], cs.at[5])
    wait_send(M4.at[: n_loc - 1], cs.at[6])
    wait_send(IS1.at[: n_loc - 1], cs.at[7])
    wait_send(IS2.at[: X - 1], cs.at[8])
    wait_send(IS3.at[: Z - 1], cs.at[9])


def local(n_sub, n_loc, partials, local_schur, rigid_basis, coarse_inverse, placement, nsub, ntile, cnum):
    slots, tiles, rl, cols = partials.shape
    modes = rigid_basis.shape[1]
    subs = nsub.shape[0]
    io, ic = coarse_inverse.shape
    nb = cols // n_loc
    Z = n_sub // X
    basis = jnp.pad(rigid_basis, ((0, 0), (0, 8 - modes), (0, 0), (0, 0))).reshape(slots, 8, tiles * rl)
    vmem = lambda *shape: pltpu.VMEM(shape, F32)
    dma = lambda *shape: pltpu.SemaphoreType.DMA(shape)
    in_v = pl.BlockSpec(memory_space=pltpu.VMEM)
    in_s = pl.BlockSpec(memory_space=pltpu.SMEM)
    any_ = pl.BlockSpec(memory_space=pl.ANY)
    precond, inner = pl.pallas_call(
        functools.partial(kernel, n_sub, n_loc),
        out_shape=(
            jax.ShapeDtypeStruct(partials.shape, F32),
            jax.ShapeDtypeStruct((1, cols), F32),
        ),
        in_specs=[any_, any_, in_v, in_v, in_s, in_s, in_s, in_s],
        out_specs=(in_v, in_v),
        scratch_shapes=[
            vmem(slots, tiles, rl, cols),
            vmem(slots, tiles, rl, tiles * n_loc * rl),
            vmem(slots, tiles, rl, cols),
            vmem(slots, tiles, n_loc, rl, cols),
            vmem(slots, tiles, rl, cols),
            vmem(8, tiles, rl, cols),
            vmem(8, tiles, rl, cols),
            vmem(4, tiles, rl, cols),
            vmem(4, tiles, rl, cols),
            vmem(slots, 8, cols),
            vmem(n_loc, nb, slots * 8),
            vmem(n_loc, nb, slots * 8),
            vmem(n_sub, nb, slots * 8),
            vmem(n_sub, nb, 128),
            vmem(n_loc, nb, 128),
            vmem(slots, 8, cols),
            vmem(n_loc, io, ic),
            vmem(n_loc * ic, 128),
            vmem(subs + slots, 8, 128),
            vmem(n_loc, rl // 2, cols),
            vmem(X, rl // 2, cols),
            vmem(Z, rl // 2, cols),
            vmem(rl, cols),
            dma(2),
            dma(4),
            dma(4),
            dma(10),
            dma(10),
            pltpu.SemaphoreType.DMA,
            dma(slots),
            dma(slots),
            dma(slots),
            dma(slots),
            dma(slots),
        ],
        compiler_params=pltpu.CompilerParams(
            collective_id=0, has_side_effects=True, vmem_limit_bytes=56 * 1024 * 1024
        ),
    )(partials, local_schur, basis, coarse_inverse, placement, nsub.T, ntile.T, cnum)
    return precond, inner.reshape(cols)


def solution(mesh):
    n_sub, n_loc = mesh.shape["sub"], mesh.shape["loc"]
    return jax.shard_map(
        functools.partial(local, n_sub, n_loc),
        mesh=mesh,
        in_specs=(
            P("sub", None, "loc", None),
            P("sub", None, "loc", None),
            P("sub", None, None, "loc"),
            P("sub", "loc"),
            P(),
            P(),
            P(),
            P(),
        ),
        out_specs=(P("sub", None, "loc", None), P()),
        check_vma=False,
    )
```

```python
import functools
import jax
import jax.numpy as jnp
from jax import lax
from jax.experimental import pallas as pl
from jax.experimental.pallas import tpu as pltpu
from jax.sharding import PartitionSpec as P

SLAB = 4
EARLY = 6
LAG = 4
MV_AT = 12
X = 4
MESH = pl.DeviceIdType.MESH
HI = lax.Precision.HIGHEST
F32 = jnp.float32
BF16 = jnp.bfloat16


def dot(a, b, dims=(((1,), (0,)), ((), ()))):
    return lax.dot_general(a, b, dims, precision=HI, preferred_element_type=F32)


def split3(v):
    h = v.astype(BF16)
    r = v - h.astype(F32)
    m = r.astype(BF16)
    return h, m, (r - m.astype(F32)).astype(BF16)


def mul16(a, b):
    return lax.dot_general(a, b, (((1,), (0,)), ((), ())), preferred_element_type=F32)


def stacked_dot(a, b):
    n = a.shape[0]
    ah, am, al = split3(a)
    bh, bm, bl = split3(b)
    one = mul16(jnp.concatenate([ah, am, al], axis=0), bh)
    two = mul16(jnp.concatenate([ah, am], axis=0), bm)
    low = one[2 * n :] + two[n:] + mul16(ah, bl)
    return one[:n] + (one[n : 2 * n] + two[:n] + low)


def kernel(
    n_sub,
    n_loc,
    part_hbm,
    schur_hbm,
    basis_hbm,
    inv_hbm,
    placement_hbm,
    nsub_hbm,
    ntile_hbm,
    cnum_hbm,
    out,
    inner_out,
    basis_in,
    inv,
    placement,
    nsub,
    ntile,
    cnum,
    basis,
    OUT,
    PV,
    SV,
    SC,
    G,
    V,
    H1,
    H2,
    SB1,
    SB2,
    CPP,
    CP,
    CT,
    R1,
    R2,
    R3,
    M4,
    MV,
    IF,
    IT,
    W,
    IS1,
    IS2,
    IS3,
    ACC,
    ld,
    relay,
    od,
    ir,
    hs,
    hr,
    cs,
    cr,
    ysend,
    ra,
    rb,
    ha,
    hb,
    rs,
):
    Z = n_sub // X
    Y = n_loc // 2
    slots, tiles, rl, cols = PV.shape
    subs = nsub.shape[1]
    rows_here = tiles * rl
    modes = 6
    pad = 8
    nb = cols // n_loc
    io, ic = inv.shape

    o = lax.axis_index("sub")
    l = lax.axis_index("loc")
    z, x = o // X, o % X
    y, c = l // 2, l % 2
    lp = 2 * ((y + 1) % Y) + c
    lm = 2 * ((y + Y - 1) % Y) + c
    l2 = 2 * ((y + 2) % Y) + c
    sib = 2 * y + (1 - c)
    right, left = (o + 1) % n_sub, (o + n_sub - 1) % n_sub

    def rcopy(src, dst, send, recv, dev):
        return pltpu.make_async_remote_copy(
            src_ref=src, dst_ref=dst, send_sem=send, recv_sem=recv, device_id=dev, device_id_type=MESH
        )

    def wait_recv(ref, sem):
        rcopy(ref, ref, sem, sem, (o, sib)).wait_recv()

    def wait_send(ref, sem):
        rcopy(ref, ref, sem, sem, (o, sib)).wait_send()

    pairs = [(placement_hbm, placement), (nsub_hbm, nsub), (ntile_hbm, ntile), (part_hbm, PV)]
    pairs += [(inv_hbm, inv), (basis_hbm, basis_in), (cnum_hbm, cnum), (schur_hbm, SV)]
    loads = [pltpu.make_async_copy(src, dst, ld.at[k]) for k, (src, dst) in enumerate(pairs)]
    for load in loads:
        load.start()

    barrier = pltpu.get_barrier_semaphore()
    near = [(o, lp), (o, lm), (o, sib)]
    near += [(z * X + (x + i) % X, l) for i in (1, X - 1)]
    near += [(((z + i) % Z) * X + x, l) for i in (1, Z - 1)]
    peers = near + [(right, l), (left, l)]
    for peer in peers:
        pl.semaphore_signal(barrier, inc=1, device_id=peer, device_id_type=MESH)

    circles = [near, [near[2]] + near[5:], near[5:]]

    def tell(k):
        for peer in circles[k]:
            pl.semaphore_signal(relay.at[k], inc=1, device_id=peer, device_id_type=MESH)

    def heard(k):
        pl.semaphore_wait(relay.at[k], len(circles[k]))

    def load_of(i):
        return placement[i] + (SLAB - 1)

    for load in loads[:3]:
        load.wait()
    start = lax.fori_loop(
        0, n_sub, lambda i, acc: acc + jnp.where(i < o, load_of(i), 0), jnp.int32(0)
    )
    cnt = load_of(o)

    def slot_of(p):
        inner = jnp.where(p < 4, 4 + p, p - 4)
        at_left, at_right = (p >= 4) & (p < 8), (p >= 8) & (p < 12)
        j_right = cnt - 12 + p
        slot = jnp.where(at_right, j_right, jnp.where(at_left, p - 4, inner))
        live = jnp.where(at_right, j_right >= 4, at_left | (inner < cnt - 4))
        return jnp.clip(slot, 0, slots - 1), live

    def pos_of(j):
        p = jnp.where(
            j < 4,
            4 + j,
            jnp.where(j >= cnt - 4, 8 + j - (cnt - 4), jnp.where(j < 8, j - 4, j + 4)),
        )
        return jnp.clip(p, 0, slots - 1)

    def link(j, live, t):
        sid = jnp.clip(start + j, 0, subs - 1)
        partner = nsub[t, sid]
        mate = jnp.clip(ntile[t, sid], 0, tiles - 1)
        linked = (partner >= 0) & live
        q = partner - start
        own = (q >= 0) & (q < cnt)
        hq = jnp.clip(jnp.where(q < 0, 4 + q, 4 + q - cnt), 0, 7)
        return linked, own, jnp.clip(q, 0, slots - 1), hq, mate

    def residual(p, halo):
        j, live = slot_of(p)
        for t in range(tiles):
            linked, own, q, hq, mt = link(j, live, t)
            other = PV[q, mt]
            if halo:
                other = jnp.where(own, other, H1[hq, mt])
            res = PV[j, t] + jnp.where(linked, other, 0.0)
            w = jnp.where(linked, 0.5, 1.0)
            val = jnp.where(live, w * res, 0.0)
            SC[p, t] = val
            G[p, t, l] = val

    def coarse_part(p):
        j, _ = slot_of(p)
        CPP[p] = dot(basis[j], SC[p].reshape(rows_here, cols))

    def send_own(p):
        src = SC.at[p]
        dst = G.at[p, :, l]
        rcopy(src, dst, ysend, ra.at[p], (o, lp)).start()
        rcopy(src, dst, ysend, rb.at[p], (o, lm)).start()
        rcopy(src, dst, ysend, rs.at[p], (o, sib)).start()

    def forward(p):
        wait_recv(G.at[p, :, lm], ra.at[p])
        half = G.at[p, : tiles // 2, lm]
        rcopy(half, half, ysend, ha.at[p], (o, lp)).start()
        whole = G.at[p, :, lm]
        rcopy(whole, whole, ysend, rs.at[p], (o, sib)).start()
        wait_recv(G.at[p, :, lp], rb.at[p])
        half = G.at[p, tiles // 2 :, lp]
        rcopy(half, half, ysend, hb.at[p], (o, lm)).start()
        whole = G.at[p, :, lp]
        rcopy(whole, whole, ysend, rs.at[p], (o, sib)).start()

    def halves(p):
        wait_recv(G.at[p, : tiles // 2, l2], ha.at[p])
        wait_recv(G.at[p, tiles // 2 :, l2], hb.at[p])
        whole = G.at[p, :, l2]
        rcopy(whole, whole, ysend, rs.at[p], (o, sib)).start()

    def apply_local(p):
        wait_recv(G.at[p, :, : n_loc // 2], rs.at[p])
        j, _ = slot_of(p)
        a = SV[j].reshape(rows_here, tiles * n_loc * rl)
        b = G[p].reshape(tiles * n_loc * rl, cols)
        V[p] = dot(a, b).reshape(tiles, rl, cols)

    def correct(p):
        j, live = slot_of(p)
        corr = dot(basis[j], MV[j], (((0,), (0,)), ((), ())))
        val = V[p] + corr.reshape(tiles, rl, cols)
        acc = ACC[...]
        for t in range(tiles):
            linked, _, _, _, _ = link(j, live, t)
            w = jnp.where(linked, 0.5, 1.0)
            acc = acc + SC[p, t] * val[t]
            V[p, t] = jnp.where(live, w * val[t], 0.0)
        ACC[...] = acc

    def loc_spread(src_of, buf, k):
        for i in range(1, n_loc):
            peer = (l + i) % n_loc
            rcopy(src_of(peer), buf.at[l], cs.at[k], cr.at[k], (o, peer)).start()

    def loc_wait(buf, k):
        wait_recv(buf.at[: n_loc - 1], cr.at[k])

    def x_spread(buf, k):
        for i in range(1, X):
            peer = z * X + (x + i) % X
            rcopy(buf.at[o], buf.at[o], cs.at[k], cr.at[k], (peer, l)).start()

    def x_wait(buf, k):
        wait_recv(buf.at[: X - 1], cr.at[k])

    def z_spread(buf, k):
        block = buf.at[pl.ds(z * X, X)]
        for i in range(1, Z):
            peer = ((z + i) % Z) * X + x
            rcopy(block, block, cs.at[k], cr.at[k], (peer, l)).start()

    def z_wait(buf, k):
        wait_recv(buf.at[: (Z - 1) * X], cr.at[k])

    loads[3].wait()

    for i in range(4):
        for t in range(tiles):
            SB1[i, t] = PV[jnp.clip(cnt - 4 + i, 0, slots - 1), t]

    pl.semaphore_wait(barrier, len(peers))

    to_left = rcopy(PV.at[:4], H1.at[4:], hs.at[0], hr.at[0], (left, l))
    to_right = rcopy(SB1, H1.at[:4], hs.at[1], hr.at[1], (right, l))
    to_left.start()
    to_right.start()
    tell(0)
    loads[4].wait()
    IF[l] = inv[...]
    for k, peer in enumerate((lp, lm, sib)):
        rcopy(inv, IF.at[l], cs.at[0], ir.at[k], (o, peer)).start()

    def first(p, carry):
        residual(p, False)
        return carry

    def first_send(p, carry):
        send_own(p)
        return carry

    def second(p, carry):
        residual(p, False)
        return carry

    def second_part(p, carry):
        coarse_part(p)
        return carry

    residual(0, False)
    send_own(0)
    lax.fori_loop(1, 4, first, 0)
    heard(0)
    tell(1)
    wait_recv(IF.at[lm], ir.at[0])
    rcopy(IF.at[lm], IF.at[lm], cs.at[0], ir.at[3], (o, lp)).start()
    rcopy(IF.at[lm], IF.at[lm], cs.at[0], ir.at[4], (o, sib)).start()
    lax.fori_loop(1, 4, first_send, 0)
    wait_recv(IF.at[lp], ir.at[1])
    rcopy(IF.at[lp], IF.at[lp], cs.at[0], ir.at[5], (o, sib)).start()
    stack = slots * modes * tiles
    spread = lax.broadcasted_iota(jnp.int32, (rl, rows_here), 1) % rl
    spread = (spread == lax.broadcasted_iota(jnp.int32, (rl, rows_here), 0)).astype(F32)
    loads[5].wait()
    wide = dot(basis_in[...].reshape(stack, rl), spread)
    at_row = lax.broadcasted_iota(jnp.int32, (stack, rows_here), 0) % tiles
    at_lane = lax.broadcasted_iota(jnp.int32, (stack, rows_here), 1) // rl
    wide = jnp.where(at_row == at_lane, wide, 0.0).reshape(slots * modes, tiles, rows_here)
    wide = jnp.sum(wide, axis=1)
    basis[...] = jnp.zeros_like(basis)
    for j in range(slots):
        basis[j, :modes] = wide[j * modes : (j + 1) * modes]

    lax.fori_loop(12, 14, second, 0)
    lax.fori_loop(12, 14, first_send, 0)
    lax.fori_loop(14, 16, second, 0)
    heard(1)
    tell(2)
    wait_recv(IF.at[l2], ir.at[3])
    rcopy(IF.at[l2], IF.at[l2], cs.at[0], ir.at[6], (o, sib)).start()
    lax.fori_loop(0, 4, second_part, 0)
    lax.fori_loop(12, 16, second_part, 0)

    ACC[...] = jnp.zeros_like(ACC)
    IT[...] = jnp.zeros_like(IT)
    W[...] = jnp.zeros_like(W)
    for k in (2, 4, 5, 6):
        wait_recv(IF.at[0], ir.at[k])
    for k in range(n_loc):
        IT[k * ic : (k + 1) * ic, :io] = IF[k].T

    def fill(s, carry):
        for m in range(modes):
            row = jnp.clip(cnum[s * modes + m], 0, n_loc * ic - 1)
            W[s, m : m + 1, :] = IT[pl.ds(row, 1), :]
        return carry

    loads[6].wait()
    lax.fori_loop(0, subs, fill, 0)

    heard(2)
    to_left.wait_recv()
    to_right.wait_recv()

    def third(p, carry):
        residual(p, True)
        coarse_part(p)
        return carry

    lax.fori_loop(4, 12, third, 0)

    for j in range(slots):
        CP[j] = jnp.where(j < cnt, CPP[pos_of(jnp.int32(j))], 0.0)
    CT[...] = CP[...].reshape(slots * pad, cols).T.reshape(n_loc, nb, slots * pad)
    R1[l] = CT[l]
    loc_spread(lambda peer: CT.at[peer], R1, 1)

    def reduce_loc():
        loc_wait(R1, 1)
        total = R1[0]
        for i in range(1, n_loc):
            total = total + R1[i]
        R2[o] = total
        x_spread(R2, 2)

    def gather_z():
        x_wait(R2, 2)
        z_spread(R2, 3)

    def solve():
        z_wait(R2, 3)

        def rows_at(at):
            return W[pl.ds(jnp.clip(at, 0, subs), slots)].reshape(slots * pad, 128)

        def body(k, carry):
            total, at = carry
            later = at + load_of(2 * k)
            rhs = jnp.concatenate([R2[2 * k], R2[2 * k + 1]], axis=1)
            rows = jnp.concatenate([rows_at(at), rows_at(later)], axis=0)
            return total + stacked_dot(rhs, rows), later + load_of(2 * k + 1)

        total, _ = lax.fori_loop(0, n_sub // 2, body, (jnp.zeros((nb, 128), F32), jnp.int32(0)))
        R3[o] = total
        x_spread(R3, 4)

    def gather_z2():
        x_wait(R3, 4)
        z_spread(R3, 5)

    def select():
        z_wait(R3, 5)
        lanes = lax.broadcasted_iota(jnp.int32, (8, 128), 1)

        def number(j, v):
            sid = jnp.clip(start + j, 0, subs - 1)
            for m in range(modes):
                row = cnum[sid * modes + m]
                v = jnp.where((lanes == j * pad + m) & (j < cnt), row, v)
            return v

        numbers = lax.fori_loop(0, slots, number, jnp.full((8, 128), -1, jnp.int32))
        wanted = jnp.broadcast_to(numbers[:1], (128, 128))
        rows = lax.broadcasted_iota(jnp.int32, (128, 128), 0)

        def hot(k):
            return ((wanted == rows + k * io) & (rows < io)).astype(F32).astype(BF16)

        def body(k, total):
            v = jnp.concatenate([R3[2 * k], R3[2 * k + 1]], axis=1)
            parts = jnp.concatenate(split3(v), axis=0)
            picked = mul16(parts, jnp.concatenate([hot(2 * k), hot(2 * k + 1)], axis=0))
            return total + ((picked[2 * nb :] + picked[nb : 2 * nb]) + picked[:nb])

        mv = lax.fori_loop(0, n_sub // 2, body, jnp.zeros((nb, 128), F32))
        M4[l] = mv
        loc_spread(lambda peer: M4.at[l], M4, 6)

    def modes_ready():
        loc_wait(M4, 6)
        MV[...] = M4[...].reshape(cols, 128).T.reshape(slots, pad, cols)

        def body(p, carry):
            correct(p)
            return carry

        lax.fori_loop(4, 8, body, 0)
        rcopy(V.at[4:8], H2.at[4:], hs.at[2], hr.at[2], (left, l)).start()
        lax.fori_loop(8, MV_AT - LAG + 1, body, 0)

    def send_halo():
        for i in range(4):
            p = pos_of(cnt - 4 + i)
            for t in range(tiles):
                SB2[i, t] = V[p, t]
        rcopy(SB2, H2.at[:4], hs.at[3], hr.at[3], (right, l)).start()

    def late(p):
        def run():
            correct(p)
            correct(p + 1)

        return run

    chain = {2: reduce_loc, 3: gather_z, 5: solve, 6: gather_z2, 8: select, MV_AT: modes_ready, 11 + LAG: send_halo}
    chain.update({12 + LAG: late(0), 13 + LAG: late(2)})

    loads[7].wait()

    def step(s, carry):
        @pl.when(s < slots)
        def _():
            forward(s)

        @pl.when(s < slots - EARLY)
        def _():
            send_own(jnp.where(s < 8, s + 4, s + EARLY))

        @pl.when((s >= LAG - 1) & (s < slots + LAG - 1))
        def _():
            halves(s - (LAG - 1))

        @pl.when(s >= LAG)
        def _():
            apply_local(s - LAG)

        @pl.when(s > MV_AT)
        def _():
            correct(s - LAG)

        for at, what in chain.items():
            pl.when(s == at)(what)
        return carry

    lax.fori_loop(0, slots + LAG, step, 0)

    IS1[l] = ACC[: rl // 2, :] + ACC[rl // 2 :, :]
    loc_spread(lambda peer: IS1.at[l], IS1, 7)

    wait_recv(H2.at[4:], hr.at[2])
    wait_recv(H2.at[:4], hr.at[3])

    def put(k, a, b):
        return pltpu.make_async_copy(OUT.at[a:b], out.at[a:b], od.at[k])

    def finish(j, carry):
        live = j < cnt
        p = pos_of(j)
        for t in range(tiles):
            linked, own, q, hq, mt = link(j, live, t)
            other = jnp.where(own, V[pos_of(q), mt], H2[hq, mt])
            val = V[p, t] + jnp.where(linked, other, 0.0)
            OUT[j, t] = jnp.where(live, val, 0.0)
        return carry

    lax.fori_loop(0, 6, finish, 0)
    put(0, 0, 6).start()
    loc_wait(IS1, 7)
    total = IS1[0]
    for i in range(1, n_loc):
        total = total + IS1[i]
    IS2[x] = total
    for i in range(1, X):
        peer = z * X + (x + i) % X
        rcopy(IS2.at[x], IS2.at[x], cs.at[8], cr.at[8], (peer, l)).start()
    lax.fori_loop(6, 11, finish, 0)
    put(1, 6, 11).start()
    wait_recv(IS2.at[: X - 1], cr.at[8])
    total = IS2[0]
    for i in range(1, X):
        total = total + IS2[i]
    IS3[z] = total
    for i in range(1, Z):
        peer = ((z + i) % Z) * X + x
        rcopy(IS3.at[z], IS3.at[z], cs.at[9], cr.at[9], (peer, l)).start()
    lax.fori_loop(11, 16, finish, 0)
    put(2, 11, 16).start()
    wait_recv(IS3.at[: Z - 1], cr.at[9])
    total = IS3[0]
    for i in range(1, Z):
        total = total + IS3[i]
    inner_out[...] = jnp.sum(total, axis=0, keepdims=True)

    put(0, 0, 6).wait()
    put(1, 6, 11).wait()
    put(2, 11, 16).wait()
    wait_send(PV.at[:4], hs.at[0])
    wait_send(SB1, hs.at[1])
    wait_send(V.at[4:8], hs.at[2])
    wait_send(SB2, hs.at[3])
    wait_send(G.at[:, :, : n_loc - 1], ysend)
    wait_send(IF.at[: n_loc - 1], cs.at[0])
    wait_send(R1.at[: n_loc - 1], cs.at[1])
    wait_send(R2.at[: X - 1], cs.at[2])
    wait_send(R2.at[: (Z - 1) * X], cs.at[3])
    wait_send(R3.at[: X - 1], cs.at[4])
    wait_send(R3.at[: (Z - 1) * X], cs.at[5])
    wait_send(M4.at[: n_loc - 1], cs.at[6])
    wait_send(IS1.at[: n_loc - 1], cs.at[7])
    wait_send(IS2.at[: X - 1], cs.at[8])
    wait_send(IS3.at[: Z - 1], cs.at[9])


def local(n_sub, n_loc, partials, local_schur, rigid_basis, coarse_inverse, placement, nsub, ntile, cnum):
    slots, tiles, rl, cols = partials.shape
    modes = rigid_basis.shape[1]
    subs = nsub.shape[0]
    io, ic = coarse_inverse.shape
    nb = cols // n_loc
    Z = n_sub // X
    vmem = lambda *shape: pltpu.VMEM(shape, F32)
    dma = lambda *shape: pltpu.SemaphoreType.DMA(shape)
    in_v = pl.BlockSpec(memory_space=pltpu.VMEM)
    hbm = pl.BlockSpec(memory_space=pltpu.HBM)
    any_ = pl.BlockSpec(memory_space=pl.ANY)
    precond, inner = pl.pallas_call(
        functools.partial(kernel, n_sub, n_loc),
        out_shape=(
            jax.ShapeDtypeStruct(partials.shape, F32),
            jax.ShapeDtypeStruct((1, cols), F32),
        ),
        in_specs=[hbm] * 8,
        out_specs=(any_, in_v),
        scratch_shapes=[
            vmem(*rigid_basis.shape),
            vmem(io, ic),
            pltpu.SMEM(placement.shape, jnp.int32),
            pltpu.SMEM(nsub.shape[::-1], jnp.int32),
            pltpu.SMEM(ntile.shape[::-1], jnp.int32),
            pltpu.SMEM(cnum.shape, jnp.int32),
            vmem(slots, 8, tiles * rl),
            vmem(slots, tiles, rl, cols),
            vmem(slots, tiles, rl, cols),
            vmem(slots, tiles, rl, tiles * n_loc * rl),
            vmem(slots, tiles, rl, cols),
            vmem(slots, tiles, n_loc, rl, cols),
            vmem(slots, tiles, rl, cols),
            vmem(8, tiles, rl, cols),
            vmem(8, tiles, rl, cols),
            vmem(4, tiles, rl, cols),
            vmem(4, tiles, rl, cols),
            vmem(slots, 8, cols),
            vmem(slots, 8, cols),
            vmem(n_loc, nb, slots * 8),
            vmem(n_loc, nb, slots * 8),
            vmem(n_sub, nb, slots * 8),
            vmem(n_sub, nb, 128),
            vmem(n_loc, nb, 128),
            vmem(slots, 8, cols),
            vmem(n_loc, io, ic),
            vmem(n_loc * ic, 128),
            vmem(subs + slots, 8, 128),
            vmem(n_loc, rl // 2, cols),
            vmem(X, rl // 2, cols),
            vmem(Z, rl // 2, cols),
            vmem(rl, cols),
            dma(8),
            pltpu.SemaphoreType.REGULAR((3,)),
            dma(3),
            dma(7),
            dma(4),
            dma(4),
            dma(10),
            dma(10),
            pltpu.SemaphoreType.DMA,
            dma(slots),
            dma(slots),
            dma(slots),
            dma(slots),
            dma(slots),
        ],
        compiler_params=pltpu.CompilerParams(
            collective_id=0, has_side_effects=True, vmem_limit_bytes=56 * 1024 * 1024
        ),
    )(partials, local_schur, rigid_basis, coarse_inverse, placement, nsub.T, ntile.T, cnum)
    return precond, inner.reshape(cols)


def solution(mesh):
    n_sub, n_loc = mesh.shape["sub"], mesh.shape["loc"]
    return jax.shard_map(
        functools.partial(local, n_sub, n_loc),
        mesh=mesh,
        in_specs=(
            P("sub", None, "loc", None),
            P("sub", None, "loc", None),
            P("sub", None, None, "loc"),
            P("sub", "loc"),
            P(),
            P(),
            P(),
            P(),
        ),
        out_specs=(P("sub", None, "loc", None), P()),
        check_vma=False,
    )
```

```python
import functools
import jax
import jax.numpy as jnp
from jax import lax
from jax.experimental import pallas as pl
from jax.experimental.pallas import tpu as pltpu
from jax.sharding import PartitionSpec as P

SLAB = 4
EARLY = 5
LAG = 4
MV_AT = 13
CUTS = ((0, 6), (6, 12), (12, 16))
X = 4
MESH = pl.DeviceIdType.MESH
HI = lax.Precision.HIGHEST
F32 = jnp.float32
BF16 = jnp.bfloat16


def dot(a, b, dims=(((1,), (0,)), ((), ()))):
    return lax.dot_general(a, b, dims, precision=HI, preferred_element_type=F32)


def split3(v):
    h = v.astype(BF16)
    r = v - h.astype(F32)
    m = r.astype(BF16)
    return h, m, (r - m.astype(F32)).astype(BF16)


def mul16(a, b):
    return lax.dot_general(a, b, (((1,), (0,)), ((), ())), preferred_element_type=F32)


def stacked_dot(a, b):
    n = a.shape[0]
    ah, am, al = split3(a)
    bh, bm, bl = split3(b)
    one = mul16(jnp.concatenate([ah, am, al], axis=0), bh)
    two = mul16(jnp.concatenate([ah, am], axis=0), bm)
    low = one[2 * n :] + two[n:] + mul16(ah, bl)
    return one[:n] + (one[n : 2 * n] + two[:n] + low)


def kernel(
    n_sub,
    n_loc,
    part_hbm,
    schur_hbm,
    basis_hbm,
    inv_hbm,
    placement_hbm,
    nsub_hbm,
    ntile_hbm,
    cnum_hbm,
    out,
    inner_out,
    basis_in,
    inv,
    placement,
    nsub,
    ntile,
    cnum,
    basis,
    OUT,
    PV,
    SV,
    SC,
    G,
    V,
    H1,
    H2,
    SB1,
    SB2,
    CPP,
    CP,
    CT,
    R1,
    R2,
    R3,
    M4,
    MV,
    IF,
    IT,
    W,
    IS1,
    IS2,
    IS3,
    ACC,
    ld,
    relay,
    od,
    ir,
    hs,
    hr,
    cs,
    cr,
    ysend,
    ra,
    rb,
    ha,
    hb,
    rs,
):
    Z = n_sub // X
    Y = n_loc // 2
    slots, tiles, rl, cols = PV.shape
    subs = nsub.shape[1]
    rows_here = tiles * rl
    modes = 6
    pad = 8
    nb = cols // n_loc
    io, ic = inv.shape

    o = lax.axis_index("sub")
    l = lax.axis_index("loc")
    z, x = o // X, o % X
    y, c = l // 2, l % 2
    lp = 2 * ((y + 1) % Y) + c
    lm = 2 * ((y + Y - 1) % Y) + c
    l2 = 2 * ((y + 2) % Y) + c
    sib = 2 * y + (1 - c)
    right, left = (o + 1) % n_sub, (o + n_sub - 1) % n_sub

    def rcopy(src, dst, send, recv, dev):
        return pltpu.make_async_remote_copy(
            src_ref=src, dst_ref=dst, send_sem=send, recv_sem=recv, device_id=dev, device_id_type=MESH
        )

    def wait_recv(ref, sem):
        rcopy(ref, ref, sem, sem, (o, sib)).wait_recv()

    def wait_send(ref, sem):
        rcopy(ref, ref, sem, sem, (o, sib)).wait_send()

    pairs = [(placement_hbm, placement), (nsub_hbm, nsub), (ntile_hbm, ntile), (part_hbm, PV)]
    pairs += [(inv_hbm, inv), (basis_hbm, basis_in), (cnum_hbm, cnum), (schur_hbm, SV)]
    loads = [pltpu.make_async_copy(src, dst, ld.at[k]) for k, (src, dst) in enumerate(pairs)]
    for load in loads:
        load.start()

    barrier = pltpu.get_barrier_semaphore()
    near = [(o, lp), (o, lm), (o, sib)]
    near += [(z * X + (x + i) % X, l) for i in (1, X - 1)]
    near += [(((z + i) % Z) * X + x, l) for i in (1, Z - 1)]
    peers = near + [(right, l), (left, l)]
    for peer in peers:
        pl.semaphore_signal(barrier, inc=1, device_id=peer, device_id_type=MESH)

    circles = [near, [near[2]] + near[5:], near[5:]]

    def tell(k):
        for peer in circles[k]:
            pl.semaphore_signal(relay.at[k], inc=1, device_id=peer, device_id_type=MESH)

    def heard(k):
        pl.semaphore_wait(relay.at[k], len(circles[k]))

    def load_of(i):
        return placement[i] + (SLAB - 1)

    for load in loads[:3]:
        load.wait()
    start = lax.fori_loop(
        0, n_sub, lambda i, acc: acc + jnp.where(i < o, load_of(i), 0), jnp.int32(0)
    )
    cnt = load_of(o)

    def slot_of(p):
        inner = jnp.where(p < 4, 4 + p, p - 4)
        at_left, at_right = (p >= 4) & (p < 8), (p >= 8) & (p < 12)
        j_right = cnt - 12 + p
        slot = jnp.where(at_right, j_right, jnp.where(at_left, p - 4, inner))
        live = jnp.where(at_right, j_right >= 4, at_left | (inner < cnt - 4))
        return jnp.clip(slot, 0, slots - 1), live

    def pos_of(j):
        p = jnp.where(
            j < 4,
            4 + j,
            jnp.where(j >= cnt - 4, 8 + j - (cnt - 4), jnp.where(j < 8, j - 4, j + 4)),
        )
        return jnp.clip(p, 0, slots - 1)

    def link(j, live, t):
        sid = jnp.clip(start + j, 0, subs - 1)
        partner = nsub[t, sid]
        mate = jnp.clip(ntile[t, sid], 0, tiles - 1)
        linked = (partner >= 0) & live
        q = partner - start
        own = (q >= 0) & (q < cnt)
        hq = jnp.clip(jnp.where(q < 0, 4 + q, 4 + q - cnt), 0, 7)
        return linked, own, jnp.clip(q, 0, slots - 1), hq, mate

    def residual(p, halo):
        j, live = slot_of(p)
        for t in range(tiles):
            linked, own, q, hq, mt = link(j, live, t)
            other = PV[q, mt]
            if halo:
                other = jnp.where(own, other, H1[hq, mt])
            res = PV[j, t] + jnp.where(linked, other, 0.0)
            w = jnp.where(linked, 0.5, 1.0)
            val = jnp.where(live, w * res, 0.0)
            SC[p, t] = val
            G[p, t, l] = val

    def coarse_part(p):
        j, _ = slot_of(p)
        CPP[p] = dot(basis[j], SC[p].reshape(rows_here, cols))

    def send_own(p):
        src = SC.at[p]
        dst = G.at[p, :, l]
        rcopy(src, dst, ysend, ra.at[p], (o, lp)).start()
        rcopy(src, dst, ysend, rb.at[p], (o, lm)).start()
        rcopy(src, dst, ysend, rs.at[p], (o, sib)).start()

    def forward(p):
        wait_recv(G.at[p, :, lm], ra.at[p])
        half = G.at[p, : tiles // 2, lm]
        rcopy(half, half, ysend, ha.at[p], (o, lp)).start()
        whole = G.at[p, :, lm]
        rcopy(whole, whole, ysend, rs.at[p], (o, sib)).start()
        wait_recv(G.at[p, :, lp], rb.at[p])
        half = G.at[p, tiles // 2 :, lp]
        rcopy(half, half, ysend, hb.at[p], (o, lm)).start()
        whole = G.at[p, :, lp]
        rcopy(whole, whole, ysend, rs.at[p], (o, sib)).start()

    def halves(p):
        wait_recv(G.at[p, : tiles // 2, l2], ha.at[p])
        wait_recv(G.at[p, tiles // 2 :, l2], hb.at[p])
        whole = G.at[p, :, l2]
        rcopy(whole, whole, ysend, rs.at[p], (o, sib)).start()

    def apply_local(p):
        wait_recv(G.at[p, :, : n_loc // 2], rs.at[p])
        j, _ = slot_of(p)
        a = SV[j].reshape(rows_here, tiles * n_loc * rl)
        b = G[p].reshape(tiles * n_loc * rl, cols)
        V[p] = dot(a, b).reshape(tiles, rl, cols)

    def correct(p):
        j, live = slot_of(p)
        corr = dot(basis[j], MV[j], (((0,), (0,)), ((), ())))
        val = V[p] + corr.reshape(tiles, rl, cols)
        acc = ACC[...]
        for t in range(tiles):
            linked, _, _, _, _ = link(j, live, t)
            w = jnp.where(linked, 0.5, 1.0)
            acc = acc + SC[p, t] * val[t]
            V[p, t] = jnp.where(live, w * val[t], 0.0)
        ACC[...] = acc

    def loc_spread(src_of, buf, k):
        for i in range(1, n_loc):
            peer = (l + i) % n_loc
            rcopy(src_of(peer), buf.at[l], cs.at[k], cr.at[k], (o, peer)).start()

    def loc_wait(buf, k):
        wait_recv(buf.at[: n_loc - 1], cr.at[k])

    def x_spread(buf, k):
        for i in range(1, X):
            peer = z * X + (x + i) % X
            rcopy(buf.at[o], buf.at[o], cs.at[k], cr.at[k], (peer, l)).start()

    def x_wait(buf, k):
        wait_recv(buf.at[: X - 1], cr.at[k])

    def z_spread(buf, k):
        block = buf.at[pl.ds(z * X, X)]
        for i in range(1, Z):
            peer = ((z + i) % Z) * X + x
            rcopy(block, block, cs.at[k], cr.at[k], (peer, l)).start()

    def z_wait(buf, k):
        wait_recv(buf.at[: (Z - 1) * X], cr.at[k])

    loads[3].wait()

    for i in range(4):
        for t in range(tiles):
            SB1[i, t] = PV[jnp.clip(cnt - 4 + i, 0, slots - 1), t]

    pl.semaphore_wait(barrier, len(peers))

    to_left = rcopy(PV.at[:4], H1.at[4:], hs.at[0], hr.at[0], (left, l))
    to_right = rcopy(SB1, H1.at[:4], hs.at[1], hr.at[1], (right, l))
    to_left.start()
    to_right.start()
    tell(0)
    loads[4].wait()
    IF[l] = inv[...]
    for k, peer in enumerate((lp, lm, sib)):
        rcopy(inv, IF.at[l], cs.at[0], ir.at[k], (o, peer)).start()

    def first(p, carry):
        residual(p, False)
        return carry

    def first_send(p, carry):
        send_own(p)
        return carry

    def second(p, carry):
        residual(p, False)
        return carry

    def second_part(p, carry):
        coarse_part(p)
        return carry

    residual(0, False)
    send_own(0)
    lax.fori_loop(1, 4, first, 0)
    heard(0)
    tell(1)
    wait_recv(IF.at[lm], ir.at[0])
    rcopy(IF.at[lm], IF.at[lm], cs.at[0], ir.at[3], (o, lp)).start()
    rcopy(IF.at[lm], IF.at[lm], cs.at[0], ir.at[4], (o, sib)).start()
    lax.fori_loop(1, 4, first_send, 0)
    wait_recv(IF.at[lp], ir.at[1])
    rcopy(IF.at[lp], IF.at[lp], cs.at[0], ir.at[5], (o, sib)).start()
    stack = slots * modes * tiles
    spread = lax.broadcasted_iota(jnp.int32, (rl, rows_here), 1) % rl
    spread = (spread == lax.broadcasted_iota(jnp.int32, (rl, rows_here), 0)).astype(F32)
    loads[5].wait()
    wide = dot(basis_in[...].reshape(stack, rl), spread)
    at_row = lax.broadcasted_iota(jnp.int32, (stack, rows_here), 0) % tiles
    at_lane = lax.broadcasted_iota(jnp.int32, (stack, rows_here), 1) // rl
    wide = jnp.where(at_row == at_lane, wide, 0.0).reshape(slots * modes, tiles, rows_here)
    wide = jnp.sum(wide, axis=1)
    basis[...] = jnp.zeros_like(basis)
    for j in range(slots):
        basis[j, :modes] = wide[j * modes : (j + 1) * modes]

    lax.fori_loop(12, 13, second, 0)
    lax.fori_loop(12, 13, first_send, 0)
    lax.fori_loop(13, 16, second, 0)
    heard(1)
    tell(2)
    wait_recv(IF.at[l2], ir.at[3])
    rcopy(IF.at[l2], IF.at[l2], cs.at[0], ir.at[6], (o, sib)).start()
    lax.fori_loop(0, 4, second_part, 0)
    lax.fori_loop(12, 16, second_part, 0)

    ACC[...] = jnp.zeros_like(ACC)
    IT[...] = jnp.zeros_like(IT)
    W[...] = jnp.zeros_like(W)
    for k in (2, 4, 5, 6):
        wait_recv(IF.at[0], ir.at[k])
    for k in range(n_loc):
        IT[k * ic : (k + 1) * ic, :io] = IF[k].T

    def fill(s, carry):
        for m in range(modes):
            row = jnp.clip(cnum[s * modes + m], 0, n_loc * ic - 1)
            W[s, m : m + 1, :] = IT[pl.ds(row, 1), :]
        return carry

    loads[6].wait()
    lax.fori_loop(0, subs, fill, 0)

    heard(2)
    to_left.wait_recv()
    to_right.wait_recv()

    def third(p, carry):
        residual(p, True)
        coarse_part(p)
        return carry

    lax.fori_loop(4, 12, third, 0)

    for j in range(slots):
        CP[j] = jnp.where(j < cnt, CPP[pos_of(jnp.int32(j))], 0.0)
    CT[...] = CP[...].reshape(slots * pad, cols).T.reshape(n_loc, nb, slots * pad)
    R1[l] = CT[l]
    loc_spread(lambda peer: CT.at[peer], R1, 1)

    def reduce_loc():
        loc_wait(R1, 1)
        total = R1[0]
        for i in range(1, n_loc):
            total = total + R1[i]
        R2[o] = total
        x_spread(R2, 2)

    def gather_z():
        x_wait(R2, 2)
        z_spread(R2, 3)

    def solve():
        z_wait(R2, 3)

        def rows_at(at):
            return W[pl.ds(jnp.clip(at, 0, subs), slots)].reshape(slots * pad, 128)

        def body(k, carry):
            total, at = carry
            later = at + load_of(2 * k)
            rhs = jnp.concatenate([R2[2 * k], R2[2 * k + 1]], axis=1)
            rows = jnp.concatenate([rows_at(at), rows_at(later)], axis=0)
            return total + stacked_dot(rhs, rows), later + load_of(2 * k + 1)

        total, _ = lax.fori_loop(0, n_sub // 2, body, (jnp.zeros((nb, 128), F32), jnp.int32(0)))
        R3[o] = total
        x_spread(R3, 4)

    def gather_z2():
        x_wait(R3, 4)
        z_spread(R3, 5)

    def select():
        z_wait(R3, 5)
        lanes = lax.broadcasted_iota(jnp.int32, (8, 128), 1)

        def number(j, v):
            sid = jnp.clip(start + j, 0, subs - 1)
            for m in range(modes):
                row = cnum[sid * modes + m]
                v = jnp.where((lanes == j * pad + m) & (j < cnt), row, v)
            return v

        numbers = lax.fori_loop(0, slots, number, jnp.full((8, 128), -1, jnp.int32))
        wanted = jnp.broadcast_to(numbers[:1], (128, 128))
        rows = lax.broadcasted_iota(jnp.int32, (128, 128), 0)

        def hot(k):
            return ((wanted == rows + k * io) & (rows < io)).astype(F32).astype(BF16)

        def body(k, total):
            v = jnp.concatenate([R3[2 * k], R3[2 * k + 1]], axis=1)
            parts = jnp.concatenate(split3(v), axis=0)
            picked = mul16(parts, jnp.concatenate([hot(2 * k), hot(2 * k + 1)], axis=0))
            return total + ((picked[2 * nb :] + picked[nb : 2 * nb]) + picked[:nb])

        mv = lax.fori_loop(0, n_sub // 2, body, jnp.zeros((nb, 128), F32))
        M4[l] = mv
        loc_spread(lambda peer: M4.at[l], M4, 6)

    def modes_ready():
        loc_wait(M4, 6)
        MV[...] = M4[...].reshape(cols, 128).T.reshape(slots, pad, cols)

        def body(p, carry):
            correct(p)
            return carry

        lax.fori_loop(4, 8, body, 0)
        rcopy(V.at[4:8], H2.at[4:], hs.at[2], hr.at[2], (left, l)).start()
        lax.fori_loop(8, MV_AT - LAG + 1, body, 0)

    def send_halo():
        for i in range(4):
            p = pos_of(cnt - 4 + i)
            for t in range(tiles):
                SB2[i, t] = V[p, t]
        rcopy(SB2, H2.at[:4], hs.at[3], hr.at[3], (right, l)).start()

    def late(p):
        def run():
            correct(p)
            correct(p + 1)

        return run

    chain = {3: reduce_loc, 4: gather_z, 6: solve, 7: gather_z2, 9: select, MV_AT: modes_ready, 11 + LAG: send_halo}
    chain.update({12 + LAG: late(0), 13 + LAG: late(2)})

    loads[7].wait()

    def step(s, carry):
        @pl.when(s < slots)
        def _():
            forward(s)

        @pl.when(s < slots - EARLY)
        def _():
            send_own(jnp.where(s < 8, s + 4, s + EARLY))

        @pl.when((s >= LAG - 1) & (s < slots + LAG - 1))
        def _():
            halves(s - (LAG - 1))

        @pl.when(s >= LAG)
        def _():
            apply_local(s - LAG)

        @pl.when(s > MV_AT)
        def _():
            correct(s - LAG)

        for at, what in chain.items():
            pl.when(s == at)(what)
        return carry

    lax.fori_loop(0, slots + LAG, step, 0)

    IS1[l] = ACC[: rl // 2, :] + ACC[rl // 2 :, :]
    loc_spread(lambda peer: IS1.at[l], IS1, 7)


    def put(k, a, b):
        return pltpu.make_async_copy(OUT.at[a:b], out.at[a:b], od.at[k])

    def finish(j, carry):
        live = j < cnt
        p = pos_of(j)
        for t in range(tiles):
            linked, own, q, hq, mt = link(j, live, t)
            other = jnp.where(own, V[pos_of(q), mt], H2[hq, mt])
            val = V[p, t] + jnp.where(linked, other, 0.0)
            OUT[j, t] = jnp.where(live, val, 0.0)
        return carry

    loc_wait(IS1, 7)
    total = IS1[0]
    for i in range(1, n_loc):
        total = total + IS1[i]
    IS2[x] = total
    for i in range(1, X):
        peer = z * X + (x + i) % X
        rcopy(IS2.at[x], IS2.at[x], cs.at[8], cr.at[8], (peer, l)).start()
    wait_recv(IS2.at[: X - 1], cr.at[8])
    total = IS2[0]
    for i in range(1, X):
        total = total + IS2[i]
    IS3[z] = total
    for i in range(1, Z):
        peer = ((z + i) % Z) * X + x
        rcopy(IS3.at[z], IS3.at[z], cs.at[9], cr.at[9], (peer, l)).start()
    wait_recv(H2.at[4:], hr.at[2])
    wait_recv(H2.at[:4], hr.at[3])
    for k, (a, b) in enumerate(CUTS):
        lax.fori_loop(a, b, finish, 0)
        put(k, a, b).start()
    wait_recv(IS3.at[: Z - 1], cr.at[9])
    total = IS3[0]
    for i in range(1, Z):
        total = total + IS3[i]
    inner_out[...] = jnp.sum(total, axis=0, keepdims=True)

    for k, (a, b) in enumerate(CUTS):
        put(k, a, b).wait()
    wait_send(PV.at[:4], hs.at[0])
    wait_send(SB1, hs.at[1])
    wait_send(V.at[4:8], hs.at[2])
    wait_send(SB2, hs.at[3])
    wait_send(G.at[:, :, : n_loc - 1], ysend)
    wait_send(IF.at[: n_loc - 1], cs.at[0])
    wait_send(R1.at[: n_loc - 1], cs.at[1])
    wait_send(R2.at[: X - 1], cs.at[2])
    wait_send(R2.at[: (Z - 1) * X], cs.at[3])
    wait_send(R3.at[: X - 1], cs.at[4])
    wait_send(R3.at[: (Z - 1) * X], cs.at[5])
    wait_send(M4.at[: n_loc - 1], cs.at[6])
    wait_send(IS1.at[: n_loc - 1], cs.at[7])
    wait_send(IS2.at[: X - 1], cs.at[8])
    wait_send(IS3.at[: Z - 1], cs.at[9])


def local(n_sub, n_loc, partials, local_schur, rigid_basis, coarse_inverse, placement, nsub, ntile, cnum):
    slots, tiles, rl, cols = partials.shape
    modes = rigid_basis.shape[1]
    subs = nsub.shape[0]
    io, ic = coarse_inverse.shape
    nb = cols // n_loc
    Z = n_sub // X
    vmem = lambda *shape: pltpu.VMEM(shape, F32)
    dma = lambda *shape: pltpu.SemaphoreType.DMA(shape)
    in_v = pl.BlockSpec(memory_space=pltpu.VMEM)
    hbm = pl.BlockSpec(memory_space=pltpu.HBM)
    any_ = pl.BlockSpec(memory_space=pl.ANY)
    precond, inner = pl.pallas_call(
        functools.partial(kernel, n_sub, n_loc),
        out_shape=(
            jax.ShapeDtypeStruct(partials.shape, F32),
            jax.ShapeDtypeStruct((1, cols), F32),
        ),
        in_specs=[hbm] * 8,
        out_specs=(any_, in_v),
        scratch_shapes=[
            vmem(*rigid_basis.shape),
            vmem(io, ic),
            pltpu.SMEM(placement.shape, jnp.int32),
            pltpu.SMEM(nsub.shape[::-1], jnp.int32),
            pltpu.SMEM(ntile.shape[::-1], jnp.int32),
            pltpu.SMEM(cnum.shape, jnp.int32),
            vmem(slots, 8, tiles * rl),
            vmem(slots, tiles, rl, cols),
            vmem(slots, tiles, rl, cols),
            vmem(slots, tiles, rl, tiles * n_loc * rl),
            vmem(slots, tiles, rl, cols),
            vmem(slots, tiles, n_loc, rl, cols),
            vmem(slots, tiles, rl, cols),
            vmem(8, tiles, rl, cols),
            vmem(8, tiles, rl, cols),
            vmem(4, tiles, rl, cols),
            vmem(4, tiles, rl, cols),
            vmem(slots, 8, cols),
            vmem(slots, 8, cols),
            vmem(n_loc, nb, slots * 8),
            vmem(n_loc, nb, slots * 8),
            vmem(n_sub, nb, slots * 8),
            vmem(n_sub, nb, 128),
            vmem(n_loc, nb, 128),
            vmem(slots, 8, cols),
            vmem(n_loc, io, ic),
            vmem(n_loc * ic, 128),
            vmem(subs + slots, 8, 128),
            vmem(n_loc, rl // 2, cols),
            vmem(X, rl // 2, cols),
            vmem(Z, rl // 2, cols),
            vmem(rl, cols),
            dma(8),
            pltpu.SemaphoreType.REGULAR((3,)),
            dma(3),
            dma(7),
            dma(4),
            dma(4),
            dma(10),
            dma(10),
            pltpu.SemaphoreType.DMA,
            dma(slots),
            dma(slots),
            dma(slots),
            dma(slots),
            dma(slots),
        ],
        compiler_params=pltpu.CompilerParams(
            collective_id=0, has_side_effects=True, vmem_limit_bytes=56 * 1024 * 1024
        ),
    )(partials, local_schur, rigid_basis, coarse_inverse, placement, nsub.T, ntile.T, cnum)
    return precond, inner.reshape(cols)


def solution(mesh):
    n_sub, n_loc = mesh.shape["sub"], mesh.shape["loc"]
    return jax.shard_map(
        functools.partial(local, n_sub, n_loc),
        mesh=mesh,
        in_specs=(
            P("sub", None, "loc", None),
            P("sub", None, "loc", None),
            P("sub", None, None, "loc"),
            P("sub", "loc"),
            P(),
            P(),
            P(),
            P(),
        ),
        out_specs=(P("sub", None, "loc", None), P()),
        check_vma=False,
    )
```

```python
import functools
import jax
import jax.numpy as jnp
from jax import lax
from jax.experimental import pallas as pl
from jax.experimental.pallas import tpu as pltpu
from jax.sharding import PartitionSpec as P

SLAB = 4
EARLY = 5
LAG = 4
MV_AT = 13
CUTS = ((0, 6), (6, 12), (12, 16))
X = 4
MESH = pl.DeviceIdType.MESH
HI = lax.Precision.HIGHEST
F32 = jnp.float32
BF16 = jnp.bfloat16


def dot(a, b, dims=(((1,), (0,)), ((), ()))):
    return lax.dot_general(a, b, dims, precision=HI, preferred_element_type=F32)


def split3(v):
    h = v.astype(BF16)
    r = v - h.astype(F32)
    m = r.astype(BF16)
    return h, m, (r - m.astype(F32)).astype(BF16)


def mul16(a, b):
    return lax.dot_general(a, b, (((1,), (0,)), ((), ())), preferred_element_type=F32)


def stacked_dot(a, b):
    n = a.shape[0]
    ah, am, al = split3(a)
    bh, bm, bl = split3(b)
    one = mul16(jnp.concatenate([ah, am, al], axis=0), bh)
    two = mul16(jnp.concatenate([ah, am], axis=0), bm)
    low = one[2 * n :] + two[n:] + mul16(ah, bl)
    return one[:n] + (one[n : 2 * n] + two[:n] + low)


def kernel(
    n_sub,
    n_loc,
    part_hbm,
    schur_hbm,
    basis_hbm,
    inv_hbm,
    placement_hbm,
    nsub_hbm,
    ntile_hbm,
    cnum_hbm,
    out,
    inner_out,
    basis_in,
    inv,
    placement,
    nsub,
    ntile,
    cnum,
    basis,
    OUT,
    PV,
    SV,
    SC,
    G,
    V,
    H1,
    H2,
    SB1,
    SB2,
    CPP,
    CP,
    CT,
    R1,
    R2,
    R3,
    M4,
    MV,
    IF,
    IT,
    W,
    IS1,
    IS2,
    IS3,
    ACC,
    ld,
    relay,
    od,
    ir,
    hs,
    hr,
    cs,
    cr,
    ysend,
    ra,
    rb,
    ha,
    hb,
    rs,
):
    Z = n_sub // X
    Y = n_loc // 2
    slots, tiles, rl, cols = PV.shape
    subs = nsub.shape[1]
    rows_here = tiles * rl
    modes = 6
    pad = 8
    nb = cols // n_loc
    io, ic = inv.shape

    o = lax.axis_index("sub")
    l = lax.axis_index("loc")
    z, x = o // X, o % X
    y, c = l // 2, l % 2
    lp = 2 * ((y + 1) % Y) + c
    lm = 2 * ((y + Y - 1) % Y) + c
    l2 = 2 * ((y + 2) % Y) + c
    sib = 2 * y + (1 - c)
    right, left = (o + 1) % n_sub, (o + n_sub - 1) % n_sub

    def rcopy(src, dst, send, recv, dev):
        return pltpu.make_async_remote_copy(
            src_ref=src, dst_ref=dst, send_sem=send, recv_sem=recv, device_id=dev, device_id_type=MESH
        )

    def wait_recv(ref, sem):
        rcopy(ref, ref, sem, sem, (o, sib)).wait_recv()

    def wait_send(ref, sem):
        rcopy(ref, ref, sem, sem, (o, sib)).wait_send()

    pairs = [(placement_hbm, placement), (nsub_hbm, nsub), (ntile_hbm, ntile), (part_hbm, PV)]
    pairs += [(inv_hbm, inv), (basis_hbm, basis_in), (cnum_hbm, cnum), (schur_hbm, SV)]
    loads = [pltpu.make_async_copy(src, dst, ld.at[k]) for k, (src, dst) in enumerate(pairs)]
    for load in loads:
        load.start()

    barrier = pltpu.get_barrier_semaphore()
    near = [(o, lp), (o, lm), (o, sib)]
    near += [(z * X + (x + i) % X, l) for i in (1, X - 1)]
    near += [(((z + i) % Z) * X + x, l) for i in (1, Z - 1)]
    peers = near + [(right, l), (left, l)]
    for peer in peers:
        pl.semaphore_signal(barrier, inc=1, device_id=peer, device_id_type=MESH)

    circles = [near, [near[2]] + near[5:], near[5:]]

    def tell(k):
        for peer in circles[k]:
            pl.semaphore_signal(relay.at[k], inc=1, device_id=peer, device_id_type=MESH)

    def heard(k):
        pl.semaphore_wait(relay.at[k], len(circles[k]))

    def load_of(i):
        return placement[i] + (SLAB - 1)

    for load in loads[:3]:
        load.wait()
    start = lax.fori_loop(
        0, n_sub, lambda i, acc: acc + jnp.where(i < o, load_of(i), 0), jnp.int32(0)
    )
    cnt = load_of(o)

    def slot_of(p):
        inner = jnp.where(p < 4, 4 + p, p - 4)
        at_left, at_right = (p >= 4) & (p < 8), (p >= 8) & (p < 12)
        j_right = cnt - 12 + p
        slot = jnp.where(at_right, j_right, jnp.where(at_left, p - 4, inner))
        live = jnp.where(at_right, j_right >= 4, at_left | (inner < cnt - 4))
        return jnp.clip(slot, 0, slots - 1), live

    def pos_of(j):
        p = jnp.where(
            j < 4,
            4 + j,
            jnp.where(j >= cnt - 4, 8 + j - (cnt - 4), jnp.where(j < 8, j - 4, j + 4)),
        )
        return jnp.clip(p, 0, slots - 1)

    def link(j, live, t):
        sid = jnp.clip(start + j, 0, subs - 1)
        partner = nsub[t, sid]
        mate = jnp.clip(ntile[t, sid], 0, tiles - 1)
        linked = (partner >= 0) & live
        q = partner - start
        own = (q >= 0) & (q < cnt)
        hq = jnp.clip(jnp.where(q < 0, 4 + q, 4 + q - cnt), 0, 7)
        return linked, own, jnp.clip(q, 0, slots - 1), hq, mate

    def residual(p, halo):
        j, live = slot_of(p)
        for t in range(tiles):
            linked, own, q, hq, mt = link(j, live, t)
            other = PV[q, mt]
            if halo:
                other = jnp.where(own, other, H1[hq, mt])
            res = PV[j, t] + jnp.where(linked, other, 0.0)
            w = jnp.where(linked, 0.5, 1.0)
            val = jnp.where(live, w * res, 0.0)
            SC[p, t] = val
            G[p, t, l] = val

    def coarse_part(p):
        j, _ = slot_of(p)
        CPP[p] = dot(basis[j], SC[p].reshape(rows_here, cols))

    def send_own(p):
        src = SC.at[p]
        dst = G.at[p, :, l]
        rcopy(src, dst, ysend, ra.at[p], (o, lp)).start()
        rcopy(src, dst, ysend, rb.at[p], (o, lm)).start()
        rcopy(src, dst, ysend, rs.at[p], (o, sib)).start()

    def forward(p):
        wait_recv(G.at[p, :, lm], ra.at[p])
        half = G.at[p, : tiles // 2, lm]
        rcopy(half, half, ysend, ha.at[p], (o, lp)).start()
        whole = G.at[p, :, lm]
        rcopy(whole, whole, ysend, rs.at[p], (o, sib)).start()
        wait_recv(G.at[p, :, lp], rb.at[p])
        half = G.at[p, tiles // 2 :, lp]
        rcopy(half, half, ysend, hb.at[p], (o, lm)).start()
        whole = G.at[p, :, lp]
        rcopy(whole, whole, ysend, rs.at[p], (o, sib)).start()

    def halves(p):
        wait_recv(G.at[p, : tiles // 2, l2], ha.at[p])
        wait_recv(G.at[p, tiles // 2 :, l2], hb.at[p])
        whole = G.at[p, :, l2]
        rcopy(whole, whole, ysend, rs.at[p], (o, sib)).start()

    def apply_local(p):
        wait_recv(G.at[p, :, : n_loc // 2], rs.at[p])
        j, _ = slot_of(p)
        a = SV[j].reshape(rows_here, tiles * n_loc * rl)
        b = G[p].reshape(tiles * n_loc * rl, cols)
        V[p] = dot(a, b).reshape(tiles, rl, cols)

    def correct(p):
        j, live = slot_of(p)
        corr = dot(basis[j], MV[j], (((0,), (0,)), ((), ())))
        val = V[p] + corr.reshape(tiles, rl, cols)
        acc = ACC[...]
        for t in range(tiles):
            linked, _, _, _, _ = link(j, live, t)
            w = jnp.where(linked, 0.5, 1.0)
            acc = acc + SC[p, t] * val[t]
            V[p, t] = jnp.where(live, w * val[t], 0.0)
        ACC[...] = acc

    def loc_spread(src_of, buf, k):
        for i in range(1, n_loc):
            peer = (l + i) % n_loc
            rcopy(src_of(peer), buf.at[l], cs.at[k], cr.at[k], (o, peer)).start()

    def loc_wait(buf, k):
        wait_recv(buf.at[: n_loc - 1], cr.at[k])

    def x_spread(buf, k):
        for i in range(1, X):
            peer = z * X + (x + i) % X
            rcopy(buf.at[o], buf.at[o], cs.at[k], cr.at[k], (peer, l)).start()

    def x_wait(buf, k):
        wait_recv(buf.at[: X - 1], cr.at[k])

    def z_spread(buf, k):
        block = buf.at[pl.ds(z * X, X)]
        for i in range(1, Z):
            peer = ((z + i) % Z) * X + x
            rcopy(block, block, cs.at[k], cr.at[k], (peer, l)).start()

    def z_wait(buf, k):
        wait_recv(buf.at[: (Z - 1) * X], cr.at[k])

    loads[3].wait()

    for i in range(4):
        for t in range(tiles):
            SB1[i, t] = PV[jnp.clip(cnt - 4 + i, 0, slots - 1), t]

    pl.semaphore_wait(barrier, len(peers))

    to_left = rcopy(PV.at[:4], H1.at[4:], hs.at[0], hr.at[0], (left, l))
    to_right = rcopy(SB1, H1.at[:4], hs.at[1], hr.at[1], (right, l))
    to_left.start()
    to_right.start()
    tell(0)
    loads[4].wait()
    IF[l] = inv[...]
    for k, peer in enumerate((lp, lm, sib)):
        rcopy(inv, IF.at[l], cs.at[0], ir.at[k], (o, peer)).start()

    def first(p, carry):
        residual(p, False)
        return carry

    def first_send(p, carry):
        send_own(p)
        return carry

    def second(p, carry):
        residual(p, False)
        return carry

    def second_part(p, carry):
        coarse_part(p)
        return carry

    residual(0, False)
    send_own(0)
    lax.fori_loop(1, 4, first, 0)
    heard(0)
    tell(1)
    wait_recv(IF.at[lm], ir.at[0])
    rcopy(IF.at[lm], IF.at[lm], cs.at[0], ir.at[3], (o, lp)).start()
    rcopy(IF.at[lm], IF.at[lm], cs.at[0], ir.at[4], (o, sib)).start()
    lax.fori_loop(1, 4, first_send, 0)
    wait_recv(IF.at[lp], ir.at[1])
    rcopy(IF.at[lp], IF.at[lp], cs.at[0], ir.at[5], (o, sib)).start()
    stack = slots * modes * tiles
    spread = lax.broadcasted_iota(jnp.int32, (rl, rows_here), 1) % rl
    spread = (spread == lax.broadcasted_iota(jnp.int32, (rl, rows_here), 0)).astype(F32)
    loads[5].wait()
    wide = dot(basis_in[...].reshape(stack, rl), spread)
    at_row = lax.broadcasted_iota(jnp.int32, (stack, rows_here), 0) % tiles
    at_lane = lax.broadcasted_iota(jnp.int32, (stack, rows_here), 1) // rl
    wide = jnp.where(at_row == at_lane, wide, 0.0).reshape(slots * modes, tiles, rows_here)
    wide = jnp.sum(wide, axis=1)
    basis[...] = jnp.zeros_like(basis)
    for j in range(slots):
        basis[j, :modes] = wide[j * modes : (j + 1) * modes]

    lax.fori_loop(12, 13, second, 0)
    lax.fori_loop(12, 13, first_send, 0)
    lax.fori_loop(13, 16, second, 0)
    heard(1)
    tell(2)
    wait_recv(IF.at[l2], ir.at[3])
    rcopy(IF.at[l2], IF.at[l2], cs.at[0], ir.at[6], (o, sib)).start()
    lax.fori_loop(0, 4, second_part, 0)
    lax.fori_loop(12, 16, second_part, 0)

    ACC[...] = jnp.zeros_like(ACC)
    IT[...] = jnp.zeros_like(IT)
    W[...] = jnp.zeros_like(W)
    for k in (2, 4, 5, 6):
        wait_recv(IF.at[0], ir.at[k])
    for k in range(n_loc):
        IT[k * ic : (k + 1) * ic, :io] = IF[k].T

    def fill(s, carry):
        for m in range(modes):
            row = jnp.clip(cnum[s * modes + m], 0, n_loc * ic - 1)
            W[s, m : m + 1, :] = IT[pl.ds(row, 1), :]
        return carry

    loads[6].wait()
    lax.fori_loop(0, subs, fill, 0)

    heard(2)
    to_left.wait_recv()
    to_right.wait_recv()

    def third(p, carry):
        residual(p, True)
        coarse_part(p)
        return carry

    lax.fori_loop(4, 12, third, 0)

    for j in range(slots):
        CP[j] = jnp.where(j < cnt, CPP[pos_of(jnp.int32(j))], 0.0)
    CT[...] = CP[...].reshape(slots * pad, cols).T.reshape(n_loc, nb, slots * pad)
    R1[l] = CT[l]
    loc_spread(lambda peer: CT.at[peer], R1, 1)

    def reduce_loc():
        loc_wait(R1, 1)
        total = R1[0]
        for i in range(1, n_loc):
            total = total + R1[i]
        R2[o] = total
        x_spread(R2, 2)

    def gather_z():
        x_wait(R2, 2)
        z_spread(R2, 3)

    def solve():
        z_wait(R2, 3)

        def rows_at(at):
            return W[pl.ds(jnp.clip(at, 0, subs), slots)].reshape(slots * pad, 128)

        def body(k, carry):
            total, at = carry
            later = at + load_of(2 * k)
            rhs = jnp.concatenate([R2[2 * k], R2[2 * k + 1]], axis=1)
            rows = jnp.concatenate([rows_at(at), rows_at(later)], axis=0)
            return total + stacked_dot(rhs, rows), later + load_of(2 * k + 1)

        total, _ = lax.fori_loop(0, n_sub // 2, body, (jnp.zeros((nb, 128), F32), jnp.int32(0)))
        R3[o] = total
        x_spread(R3, 4)

    def gather_z2():
        x_wait(R3, 4)
        z_spread(R3, 5)

    def select():
        z_wait(R3, 5)
        lanes = lax.broadcasted_iota(jnp.int32, (8, 128), 1)

        def number(j, v):
            sid = jnp.clip(start + j, 0, subs - 1)
            for m in range(modes):
                row = cnum[sid * modes + m]
                v = jnp.where((lanes == j * pad + m) & (j < cnt), row, v)
            return v

        numbers = lax.fori_loop(0, slots, number, jnp.full((8, 128), -1, jnp.int32))
        wanted = jnp.broadcast_to(numbers[:1], (128, 128))
        rows = lax.broadcasted_iota(jnp.int32, (128, 128), 0)

        def hot(k):
            return ((wanted == rows + k * io) & (rows < io)).astype(F32).astype(BF16)

        def body(k, total):
            v = jnp.concatenate([R3[2 * k], R3[2 * k + 1]], axis=1)
            parts = jnp.concatenate(split3(v), axis=0)
            picked = mul16(parts, jnp.concatenate([hot(2 * k), hot(2 * k + 1)], axis=0))
            return total + ((picked[2 * nb :] + picked[nb : 2 * nb]) + picked[:nb])

        mv = lax.fori_loop(0, n_sub // 2, body, jnp.zeros((nb, 128), F32))
        M4[l] = mv
        loc_spread(lambda peer: M4.at[l], M4, 6)

    def modes_ready():
        loc_wait(M4, 6)
        MV[...] = M4[...].reshape(cols, 128).T.reshape(slots, pad, cols)

        def body(p, carry):
            correct(p)
            return carry

        lax.fori_loop(4, 8, body, 0)
        rcopy(V.at[4:8], H2.at[4:], hs.at[2], hr.at[2], (left, l)).start()
        lax.fori_loop(8, MV_AT - LAG + 1, body, 0)

    def send_halo():
        for i in range(4):
            p = pos_of(cnt - 4 + i)
            for t in range(tiles):
                SB2[i, t] = V[p, t]
        rcopy(SB2, H2.at[:4], hs.at[3], hr.at[3], (right, l)).start()

    def late(p):
        def run():
            correct(p)
            correct(p + 1)

        return run

    chain = {3: reduce_loc, 4: gather_z, 6: solve, 7: gather_z2, 9: select, MV_AT: modes_ready, 11 + LAG: send_halo}
    chain.update({12 + LAG: late(0), 13 + LAG: late(2)})

    loads[7].wait()

    def step(s, carry):
        @pl.when(s < slots)
        def _():
            forward(s)

        @pl.when(s < slots - EARLY)
        def _():
            send_own(jnp.where(s < 8, s + 4, s + EARLY))

        @pl.when((s >= LAG - 1) & (s < slots + LAG - 1))
        def _():
            halves(s - (LAG - 1))

        @pl.when(s >= LAG)
        def _():
            apply_local(s - LAG)

        @pl.when(s > MV_AT)
        def _():
            correct(s - LAG)

        for at, what in chain.items():
            pl.when(s == at)(what)
        return carry

    lax.fori_loop(0, slots + LAG, step, 0)

    IS1[l] = jnp.sum(ACC[...], axis=0, keepdims=True)
    loc_spread(lambda peer: IS1.at[l], IS1, 7)


    def put(k, a, b):
        return pltpu.make_async_copy(OUT.at[a:b], out.at[a:b], od.at[k])

    def finish(j, carry):
        live = j < cnt
        p = pos_of(j)
        for t in range(tiles):
            linked, own, q, hq, mt = link(j, live, t)
            other = jnp.where(own, V[pos_of(q), mt], H2[hq, mt])
            val = V[p, t] + jnp.where(linked, other, 0.0)
            OUT[j, t] = jnp.where(live, val, 0.0)
        return carry

    loc_wait(IS1, 7)
    total = IS1[0]
    for i in range(1, n_loc):
        total = total + IS1[i]
    IS2[x] = total
    for i in range(1, X):
        peer = z * X + (x + i) % X
        rcopy(IS2.at[x], IS2.at[x], cs.at[8], cr.at[8], (peer, l)).start()
    wait_recv(IS2.at[: X - 1], cr.at[8])
    total = IS2[0]
    for i in range(1, X):
        total = total + IS2[i]
    IS3[z] = total
    for i in range(1, Z):
        peer = ((z + i) % Z) * X + x
        rcopy(IS3.at[z], IS3.at[z], cs.at[9], cr.at[9], (peer, l)).start()
    wait_recv(H2.at[4:], hr.at[2])
    wait_recv(H2.at[:4], hr.at[3])
    for k, (a, b) in enumerate(CUTS):
        lax.fori_loop(a, b, finish, 0)
        put(k, a, b).start()
    wait_recv(IS3.at[: Z - 1], cr.at[9])
    total = IS3[0]
    for i in range(1, Z):
        total = total + IS3[i]
    inner_out[...] = total

    for k, (a, b) in enumerate(CUTS):
        put(k, a, b).wait()
    wait_send(PV.at[:4], hs.at[0])
    wait_send(SB1, hs.at[1])
    wait_send(V.at[4:8], hs.at[2])
    wait_send(SB2, hs.at[3])
    wait_send(G.at[:, :, : n_loc - 1], ysend)
    wait_send(IF.at[: n_loc - 1], cs.at[0])
    wait_send(R1.at[: n_loc - 1], cs.at[1])
    wait_send(R2.at[: X - 1], cs.at[2])
    wait_send(R2.at[: (Z - 1) * X], cs.at[3])
    wait_send(R3.at[: X - 1], cs.at[4])
    wait_send(R3.at[: (Z - 1) * X], cs.at[5])
    wait_send(M4.at[: n_loc - 1], cs.at[6])
    wait_send(IS1.at[: n_loc - 1], cs.at[7])
    wait_send(IS2.at[: X - 1], cs.at[8])
    wait_send(IS3.at[: Z - 1], cs.at[9])


def local(n_sub, n_loc, partials, local_schur, rigid_basis, coarse_inverse, placement, nsub, ntile, cnum):
    slots, tiles, rl, cols = partials.shape
    modes = rigid_basis.shape[1]
    subs = nsub.shape[0]
    io, ic = coarse_inverse.shape
    nb = cols // n_loc
    Z = n_sub // X
    vmem = lambda *shape: pltpu.VMEM(shape, F32)
    dma = lambda *shape: pltpu.SemaphoreType.DMA(shape)
    in_v = pl.BlockSpec(memory_space=pltpu.VMEM)
    hbm = pl.BlockSpec(memory_space=pltpu.HBM)
    any_ = pl.BlockSpec(memory_space=pl.ANY)
    precond, inner = pl.pallas_call(
        functools.partial(kernel, n_sub, n_loc),
        out_shape=(
            jax.ShapeDtypeStruct(partials.shape, F32),
            jax.ShapeDtypeStruct((1, cols), F32),
        ),
        in_specs=[hbm] * 8,
        out_specs=(any_, in_v),
        scratch_shapes=[
            vmem(*rigid_basis.shape),
            vmem(io, ic),
            pltpu.SMEM(placement.shape, jnp.int32),
            pltpu.SMEM(nsub.shape[::-1], jnp.int32),
            pltpu.SMEM(ntile.shape[::-1], jnp.int32),
            pltpu.SMEM(cnum.shape, jnp.int32),
            vmem(slots, 8, tiles * rl),
            vmem(slots, tiles, rl, cols),
            vmem(slots, tiles, rl, cols),
            vmem(slots, tiles, rl, tiles * n_loc * rl),
            vmem(slots, tiles, rl, cols),
            vmem(slots, tiles, n_loc, rl, cols),
            vmem(slots, tiles, rl, cols),
            vmem(8, tiles, rl, cols),
            vmem(8, tiles, rl, cols),
            vmem(4, tiles, rl, cols),
            vmem(4, tiles, rl, cols),
            vmem(slots, 8, cols),
            vmem(slots, 8, cols),
            vmem(n_loc, nb, slots * 8),
            vmem(n_loc, nb, slots * 8),
            vmem(n_sub, nb, slots * 8),
            vmem(n_sub, nb, 128),
            vmem(n_loc, nb, 128),
            vmem(slots, 8, cols),
            vmem(n_loc, io, ic),
            vmem(n_loc * ic, 128),
            vmem(subs + slots, 8, 128),
            vmem(n_loc, 1, cols),
            vmem(X, 1, cols),
            vmem(Z, 1, cols),
            vmem(rl, cols),
            dma(8),
            pltpu.SemaphoreType.REGULAR((3,)),
            dma(3),
            dma(7),
            dma(4),
            dma(4),
            dma(10),
            dma(10),
            pltpu.SemaphoreType.DMA,
            dma(slots),
            dma(slots),
            dma(slots),
            dma(slots),
            dma(slots),
        ],
        compiler_params=pltpu.CompilerParams(
            collective_id=0, has_side_effects=True, vmem_limit_bytes=56 * 1024 * 1024
        ),
    )(partials, local_schur, rigid_basis, coarse_inverse, placement, nsub.T, ntile.T, cnum)
    return precond, inner.reshape(cols)


def solution(mesh):
    n_sub, n_loc = mesh.shape["sub"], mesh.shape["loc"]
    return jax.shard_map(
        functools.partial(local, n_sub, n_loc),
        mesh=mesh,
        in_specs=(
            P("sub", None, "loc", None),
            P("sub", None, "loc", None),
            P("sub", None, None, "loc"),
            P("sub", "loc"),
            P(),
            P(),
            P(),
            P(),
        ),
        out_specs=(P("sub", None, "loc", None), P()),
        check_vma=False,
    )
```
